512 devices in a mesh: doc: 64 (over y, z), bin: 8 (over x, core).
Axes of the slice: x: 4, y: 4, z: 16, core: 2. Of those that a mesh axis runs over, the one named last changes fastest.
Arguments:
- profiles: float32 [8192, 8192], P('doc', 'bin'), may hold values from -6 to 6
- assign: int32 [8192], P('doc'), may hold values from 0 to 4095, as said below
Outputs:
- centroids: float32 [8, 512, 8192], P('bin', 'doc')
- scores: float32 [4096, 8192], P('bin', 'doc')
The draws below stay inside these ranges and needn't reach their ends.
Inputs may be any that keep to these rules, and one draw needn't show every extreme that they name: `assign`: cluster k belongs to owner (k % 512) // 8. In each aligned block of 128 documents, at most 8 documents are assigned to the clusters of one owner, and some owner has exactly 8 of them.
All inputs are finite; a program needn't handle non-finite values.
Results may differ from the reference program's by a relative error of at most 0.0029.
Values may be sent and summed in bfloat16 or wider, within the bound.
A program may use at most 64 MiB of HBM per device.

```python
import jax
import jax.numpy as jnp
from jax import lax

BINS = 8192
K = 4096
DOC_DEV = 128
DOCS = 8192
CAP = 8
OWN_CLUSTERS = 64
PART_CLUSTERS = 8
SLICE_CLUSTERS = 512
GROUPS = 8


def draw_assign(key, part):
    key = jax.random.fold_in(key, 11)
    blocks = DOCS // DOC_DEV
    key_hot, key_alt, key_perm, key_sub = jax.random.split(key, 4)
    hot_owner = jnp.minimum(jax.random.randint(key_hot, (blocks,), 0, blocks), jax.random.randint(key_alt, (blocks,), 0, blocks))
    perm_keys = jax.random.split(key_perm, blocks)
    positions = jax.vmap(lambda single: jax.random.permutation(single, DOC_DEV))(perm_keys)
    others = (positions - CAP) % (blocks - 1)
    owner_rank = jnp.where(positions < CAP, hot_owner[:, None], (hot_owner[:, None] + 1 + others) % blocks)
    local_index = jax.random.randint(key_sub, (blocks, DOC_DEV), 0, OWN_CLUSTERS)
    cluster = local_index // PART_CLUSTERS * SLICE_CLUSTERS + owner_rank * PART_CLUSTERS + local_index % PART_CLUSTERS
    return cluster.reshape(-1).astype(jnp.int32)


def steps_of(stream_key, dims, pieces, low, largest):
    loudness = 1.0
    for dim, shards_of in pieces:
        heights = jax.random.uniform(jax.random.fold_in(jax.random.fold_in(stream_key, 6), dim), (shards_of,), jnp.float32, low / len(pieces), largest / len(pieces))
        loudness = loudness * jnp.repeat(jnp.exp(heights), dims[dim] // shards_of).reshape((-1,) + (1,) * (len(dims) - 1 - dim))
    return loudness


def scatter_about(key, extent, spread, bound, cuts=(), kind=jnp.bfloat16):
    array = spread * jax.random.normal(key, extent, jnp.float32)
    if cuts:
        array = array * steps_of(key, extent, cuts, -0.22, 0.18)
    return jnp.clip(array, -bound, bound).astype(kind)


def setup_inputs(seed: int = 0) -> dict:
    key_of = jax.random.split(jax.random.key(seed), 3)
    return {
        "profiles": scatter_about(key_of[0], (DOCS, BINS), 1.0, 6.0, ((0, 64), (1, 8)), jnp.float32),
        "assign": draw_assign(jax.random.fold_in(key_of[2], 71), 0),
    }


norm_epsilon = 1e-06

def reference(profiles, assign):
    cluster_sums = jax.ops.segment_sum(profiles, assign, num_segments=K)
    squares = lax.optimization_barrier(jnp.sum(cluster_sums * cluster_sums, axis=1, keepdims=True))
    unit = cluster_sums * lax.rsqrt(squares + norm_epsilon)
    unit_low = unit.astype(jnp.bfloat16)
    profiles_low = profiles.astype(jnp.bfloat16)
    scores = lax.dot_general(unit_low, profiles_low, (((1,), (1,)), ((), ())), preferred_element_type=jnp.float32)
    return (unit.reshape(GROUPS, K // GROUPS, BINS), scores)
```

```python
import functools

import jax
import jax.numpy as jnp
from jax import lax
from jax.experimental import pallas as pl
from jax.experimental.pallas import tpu as pltpu
from jax.sharding import PartitionSpec as P

MESH = pl.DeviceIdType.MESH
EPS = 1e-06
K = 4096
DEPTH = 16
CHUNKS = 4
F32 = jnp.float32
LOW = jnp.bfloat16
NT = (((1,), (1,)), ((), ()))


def iota(shape, dim):
    return lax.broadcasted_iota(jnp.int32, shape, dim)


def kernel(
    Y, Z, B, p_ref, a_ref, cent_ref, score_ref,
    docs, own, ids, part, got, acc, sums, sum_out, sum_in, slab, sq_out, sq_in,
    nrm, fold_out, fold_in, unit,
    zr_send, zr_recv, zl_send, zl_recv, id_send, id_recv, own_send, own_recv,
    rs_send, rs_recv, sum_send, sum_recv, sq_send, sq_recv, nrm_send, nrm_recv,
    f_send, f_recv, u_send, u_recv,
):
    R, W = p_ref.shape
    NP = Z // 2
    PLANE = Y * B
    GROUP = K // B
    PART = GROUP // (Y * Z)
    OWN = PART * B
    LANES = PART * Z
    CR = R // CHUNKS
    SUB = R // B
    NC = Y * SUB
    doc, b = lax.axis_index("doc"), lax.axis_index("bin")
    y, z = doc // Z, doc % Z
    me = y * B + b

    def at_z(q):
        return (y * Z + lax.rem(z + q + Z, Z), b)

    def at_plane(idx):
        return ((idx // B) * Z + z, lax.rem(idx, B))

    def remote(src, dst, send, recv, device):
        return pltpu.make_async_remote_copy(
            src_ref=src, dst_ref=dst, send_sem=send, recv_sem=recv, device_id=device, device_id_type=MESH
        )

    def wait_bytes(ref, sem):
        pltpu.make_async_copy(ref, ref, sem).wait()

    barrier = pltpu.get_barrier_semaphore()

    @pl.loop(1, Z)
    def _(q):
        pl.semaphore_signal(barrier, inc=1, device_id=at_z(q), device_id_type=MESH)

    @pl.loop(1, PLANE)
    def _(q):
        pl.semaphore_signal(barrier, inc=1, device_id=at_plane(lax.rem(me + q, PLANE)), device_id_type=MESH)

    low = p_ref[...].astype(LOW)
    docs[0, 0:R, :] = low
    own[y] = low
    mine = jnp.broadcast_to(a_ref[...], (8, R))
    ids[0, :, 0:R] = mine
    pl.semaphore_wait(barrier, Z + PLANE - 2)

    def right(s, to, row, c):
        return remote(docs.at[s, pl.ds(c * CR, CR)], docs.at[to, pl.ds(row + c * CR, CR)],
                      zr_send.at[s, c], zr_recv.at[to, c], at_z(1))

    def left(s, row, to, c):
        return remote(docs.at[s, pl.ds(row + c * CR, CR)], docs.at[to, pl.ds(R + c * CR, CR)],
                      zl_send.at[s, c], zl_recv.at[to, c], at_z(-1))

    for c in range(CHUNKS):
        right(0, 1, 0, c).start()
        left(0, 0, 1, c).start()
    id_copies = []
    for q in range(1, Z):
        pair, half = (q % NP, int(q == NP)) if q <= NP else (Z - q, 1)
        id_copies.append(remote(
            ids.at[0, :, pl.ds(0, R)], ids.at[pair, :, pl.ds(half * R, R)],
            id_send.at[q], id_recv.at[q], at_z(q)))
        id_copies[-1].start()
    own_copies = []
    for q in range(1, Y):
        own_copies.append(remote(
            docs.at[0, pl.ds(0, R)], own.at[y], own_send.at[q], own_recv.at[q],
            (lax.rem(y + q, Y) * Z + z, b)))
        own_copies[-1].start()
    acc[...] = jnp.zeros_like(acc)
    sums[...] = jnp.zeros_like(sums)

    def partial(p):
        for v in range(Y):
            g = lax.dot_general(own[v], docs[p], NT, preferred_element_type=F32)
            part[p, :, v * SUB:(v + 1) * SUB, :] = g.reshape(B, SUB, 2 * R).astype(part.dtype)
        for q in range(1, B):
            to = lax.rem(b + q, B)
            remote(part.at[p, to], got.at[p, q - 1], rs_send.at[p], rs_recv.at[p], (doc, to)).start()

    def add_sums(p):
        a = ids[p, 0:1, :]
        rank = (a & (GROUP - 1)) // PART
        row = (rank // Z) * OWN + (a // GROUP) * PART + (a & (PART - 1))
        row = jnp.where((rank & (Z - 1)) == z, row, -1)
        hot = (iota((Y * OWN, 2 * R), 0) == row).astype(F32).astype(LOW)
        sums[...] += jnp.dot(hot, docs[p], preferred_element_type=F32)

    def fold(p, first, count):
        h = part[p, b].astype(F32)
        for i in range(B - 1):
            h += got[p, i].astype(F32)
        hi = h.astype(LOW)
        lo = (h - hi.astype(F32)).astype(LOW)
        both = jnp.concatenate([hi, lo], axis=0)
        col = jnp.transpose(jnp.broadcast_to(ids[p, 0:1, :], (128, 2 * R)))
        for g in range(first, first + count):
            hot = jnp.concatenate(
                [(col == iota((2 * R, 128), 1) + (g * GROUP + t * 128)).astype(F32).astype(LOW)
                 for t in range(GROUP // 128)], axis=1)
            d = jnp.dot(both, hot, preferred_element_type=F32)
            acc[:, g * GROUP:(g + 1) * GROUP] += d[0:NC] + d[NC:]

    def sum_copy(q):
        v = lax.rem(y + q, Y)
        return remote(sum_out.at[v], sum_in.at[q - 1], sum_send.at[q - 1], sum_recv.at[q - 1], (v * Z + z, b))

    @pl.loop(1, NP + 3)
    def _(s):
        for c in range(CHUNKS):
            early = c < CHUNKS // 2

            @pl.when(s < NP)
            def _():
                right(0, s, 0, c).wait_recv()
                go = lambda: right(s, lax.rem(s + 1, NP), jnp.where(s == NP - 1, R, 0), c).start()
                go() if early else pl.when(s < NP - 1)(go)
                left(0, 0, s, c).wait_recv()
                go_left = lambda: left(s, R, lax.rem(s + 1, NP), c).start()
                pl.when(s < NP - 1)(go_left) if early else go_left()

            @pl.when(s == NP)
            def _():
                if early:
                    right(0, 0, R, c).wait_recv()
                else:
                    left(0, 0, 0, c).wait_recv()

            if c == 0:

                @pl.when(s == 2)
                def _():
                    for copy in id_copies:
                        copy.wait()
                    for q in range(1, Y):
                        own_copies[q - 1].wait_send()
                        from_y = lax.rem(y - q + Y, Y)
                        remote(own.at[0], own.at[from_y], own_send.at[q], own_recv.at[q], (doc, b)).wait_recv()

                pl.when((s >= 2) & (s < NP + 1))(lambda: partial(s - 1))
            if c == 1:
                pl.when((s >= 2) & (s < NP + 1))(lambda: add_sums(s - 1))
            if c == 2:

                @pl.when(s == NP + 1)
                def _():
                    add_sums(0)
                    for v in range(Y):
                        sum_out[v] = sums[v * OWN:(v + 1) * OWN, :].astype(LOW)
                    for q in range(1, Y):
                        sum_copy(q).start()
                    partial(0)

            if c >= 2:

                @pl.when(s >= 3)
                def _():
                    p = lax.rem(s - 2, NP)
                    if c == 2:
                        wait_bytes(got.at[p], rs_recv.at[p])
                    half = B // 2
                    fold(p, (c - 2) * half, half)

    for g in range(B):
        fold_out[g] = acc[:, g * GROUP:(g + 1) * GROUP].astype(LOW)

    def fold_piece(idx):
        v, g = idx // B, lax.rem(idx, B)
        return (fold_out.at[g, pl.ds(pl.multiple_of(v * SUB, SUB), SUB)],
                fold_in.at[me])

    @pl.loop(1, PLANE)
    def _(q):
        idx = lax.rem(me + q, PLANE)
        src, dst = fold_piece(idx)
        remote(src, dst, f_send, f_recv, at_plane(idx)).start()

    src, dst = fold_piece(me)
    pltpu.make_async_copy(src, dst, f_recv).start()

    for q in range(1, Y):
        sum_copy(q).wait()
    total = sums[pl.ds(pl.multiple_of(y * OWN, OWN), OWN), :]
    for q in range(Y - 1):
        total += sum_in[q].astype(F32)
    slab[...] = total
    square = jnp.sum(total * total, axis=1, keepdims=True)
    square = jnp.broadcast_to(square, (OWN, 128))
    if OWN < 128:
        square = jnp.concatenate([square, jnp.zeros((128 - OWN, 128), F32)], axis=0)
    square = jnp.transpose(square)[0:8]
    sq_out[...] = square

    @pl.loop(1, PLANE)
    def _(q):
        idx = lax.rem(me + q, PLANE)
        remote(sq_out, sq_in.at[PLANE - 1 - q], sq_send, sq_recv, at_plane(idx)).start()

    wait_bytes(sq_in, sq_recv)
    sub = iota((8, 128), 0)
    lane = iota((8, 128), 1)
    table = jnp.zeros((8, 128), F32)
    for i in range(PLANE):
        row = sq_out[...] if i == PLANE - 1 else sq_in[i]
        v = lax.rem(me + i + 1, PLANE) // B
        table += jnp.where(sub == v, row, 0.0)
    inverse = lax.rsqrt(table + EPS)
    ours = jnp.sum(jnp.where(sub == y, inverse, 0.0), axis=0, keepdims=True)
    turned = pltpu.roll(inverse, lax.rem((z - b) * PART + 128, 128), 1)
    turned = jnp.where((lane >= z * PART) & (lane < (z + 1) * PART), turned, 0.0)
    nrm[Z - 1] = turned

    @pl.loop(1, Z)
    def _(q):
        remote(nrm.at[Z - 1], nrm.at[Z - 1 - q], nrm_send, nrm_recv, at_z(q)).start()

    scale = jnp.transpose(jnp.broadcast_to(ours, (128, 128)))[0:OWN]
    for t in range(W // 128):
        unit[:, t * 128:(t + 1) * 128] = slab[:, t * 128:(t + 1) * 128] * scale
    for q in range(1, B):
        to = lax.rem(b + q, B)
        remote(unit.at[pl.ds(pl.multiple_of(to * PART, PART), PART)],
               cent_ref.at[0, :, pl.ds(pl.multiple_of(b * W, W), W)],
               u_send, u_recv, (doc, to)).start()
    cent_ref[0, :, pl.ds(pl.multiple_of(b * W, W), W)] = unit[pl.ds(pl.multiple_of(b * PART, PART), PART), :]

    wait_bytes(fold_in, f_recv)
    raw = fold_in[0:B].astype(F32)
    for v in range(1, Y):
        raw += fold_in[v * B:(v + 1) * B].astype(F32)
    raw = raw.reshape(R, GROUP)
    wait_bytes(nrm.at[pl.ds(0, Z - 1)], nrm_recv)
    rows = nrm[0]
    for i in range(1, Z):
        rows += nrm[i]
    for v in range(Y):
        tile = raw[:, v * LANES:(v + 1) * LANES] * rows[v:v + 1, :]
        score_ref[v * LANES:(v + 1) * LANES, :] = jnp.transpose(tile)

    @pl.loop(0, NP)
    def _(s):
        for c in range(CHUNKS):
            early = c < CHUNKS // 2
            wait_right = lambda: right(s, s, 0, c).wait_send()
            wait_left = lambda: left(s, 0, s, c).wait_send()
            wait_right() if early else pl.when(s < NP - 1)(wait_right)
            pl.when(s < NP - 1)(wait_left) if early else wait_left()
        wait_bytes(part.at[s, pl.ds(0, B - 1)], rs_send.at[s])

    wait_bytes(fold_in.at[pl.ds(0, PLANE - 1)], f_send)
    wait_bytes(sq_in, sq_send)
    wait_bytes(nrm.at[pl.ds(0, Z - 1)], nrm_send)
    wait_bytes(cent_ref.at[0, :, pl.ds(0, (B - 1) * W)], u_send)
    wait_bytes(cent_ref.at[0, :, pl.ds(0, (B - 1) * W)], u_recv)


def program(mesh, depth, clusters):
    B = mesh.shape["bin"]
    Z = depth
    Y = mesh.shape["doc"] // Z
    NP = Z // 2
    global K
    K = clusters

    def shards(profiles, assign):
        R, W = profiles.shape
        group = clusters // B
        own = group // (Y * Z) * B
        SUB = R // B
        NC = Y * SUB
        plane = Y * B
        dma = pltpu.SemaphoreType.DMA
        scratch = [
            pltpu.VMEM((NP, 2 * R, W), LOW),
            pltpu.VMEM((Y, R, W), LOW),
            pltpu.VMEM((NP, 8, 2 * R), jnp.int32),
            pltpu.VMEM((NP, B, NC, 2 * R), F32),
            pltpu.VMEM((NP, B - 1, NC, 2 * R), F32),
            pltpu.VMEM((NC, clusters), F32),
            pltpu.VMEM((Y * own, W), F32),
            pltpu.VMEM((Y, own, W), LOW),
            pltpu.VMEM((Y - 1, own, W), LOW),
            pltpu.VMEM((own, W), F32),
            pltpu.VMEM((8, 128), F32),
            pltpu.VMEM((plane - 1, 8, 128), F32),
            pltpu.VMEM((Z, 8, 128), F32),
            pltpu.VMEM((B, NC, group), LOW),
            pltpu.VMEM((plane, SUB, group), LOW),
            pltpu.VMEM((own, W), F32),
            *[dma((NP, CHUNKS))] * 4,
            *[dma((Z,))] * 2,
            *[dma((Y,))] * 2,
            *[dma((NP,))] * 2,
            *[dma((Y - 1,))] * 2,
            *[dma] * 8,
        ]
        return pl.pallas_call(
            functools.partial(kernel, Y, Z, B),
            out_shape=(
                jax.ShapeDtypeStruct((1, group // (Y * Z), B * W), F32),
                jax.ShapeDtypeStruct((group, R), F32),
            ),
            in_specs=[pl.BlockSpec(memory_space=pltpu.VMEM)] * 2,
            out_specs=(pl.BlockSpec(memory_space=pltpu.VMEM),) * 2,
            scratch_shapes=scratch,
            compiler_params=pltpu.CompilerParams(
                collective_id=0, has_side_effects=True, vmem_limit_bytes=40 * 2**20
            ),
        )(profiles, assign.reshape(1, -1))

    return jax.shard_map(
        shards,
        mesh=mesh,
        in_specs=(P("doc", "bin"), P("doc")),
        out_specs=(P("bin", "doc", None), P("bin", "doc")),
        check_vma=False,
    )


def solution(mesh):
    return program(mesh, DEPTH, 4096)
```

```python
import functools

import jax
import jax.numpy as jnp
from jax import lax
from jax.experimental import pallas as pl
from jax.experimental.pallas import tpu as pltpu
from jax.sharding import PartitionSpec as P

MESH = pl.DeviceIdType.MESH
EPS = 1e-06
DEPTH = 16
CHUNKS = 4
F32 = jnp.float32
LOW = jnp.bfloat16
NT = (((1,), (1,)), ((), ()))


def iota(shape, dim):
    return lax.broadcasted_iota(jnp.int32, shape, dim)


def kernel(
    Y, Z, B, K, p_hbm, a_hbm, cent_ref, score_ref,
    p_ref, a_ref, docs, own, ids, col, part, got, part0, got0, part_pen, got_pen, part_last, got_last,
    acc, sums, pay_out, pay_in, sq_out, sq_in, nrm, fold_out, fold_in, cent_raw, colscale,
    in_sem, zr_send, zr_recv, zl_send, zl_recv, id_send, id_recv, own_send, own_recv,
    rs_send, rs_recv, pay_send, pay_recv, sq_send, sq_recv, nrm_send, nrm_recv,
    f_send, f_recv, u_send, u_recv,
):
    R, W = p_ref.shape
    NP = Z // 2
    LAST = NP
    PLANE = Y * B
    GROUP = K // B
    PART = GROUP // (Y * Z)
    OWN = PART * B
    LANES = PART * Z
    CR = R // CHUNKS
    SUB = R // B
    NC = Y * SUB
    CAP = 8
    doc, b = lax.axis_index("doc"), lax.axis_index("bin")
    y, z = doc // Z, doc % Z
    me = y * B + b

    def at_z(q):
        return (y * Z + lax.rem(z + q + Z, Z), b)

    def at_y(q):
        return (lax.rem(y + q, Y) * Z + z, b)

    def at_plane(idx):
        return ((idx // B) * Z + z, lax.rem(idx, B))

    def remote(src, dst, send, recv, device):
        return pltpu.make_async_remote_copy(
            src_ref=src, dst_ref=dst, send_sem=send, recv_sem=recv, device_id=device, device_id_type=MESH
        )

    def wait_bytes(ref, sem):
        pltpu.make_async_copy(ref, ref, sem).wait()

    fetch = pltpu.make_async_copy(p_hbm, p_ref, in_sem.at[0])
    fetch.start()
    fetch_ids = pltpu.make_async_copy(a_hbm, a_ref, in_sem.at[1])
    fetch_ids.start()

    barrier = pltpu.get_barrier_semaphore()

    @pl.loop(1, Z)
    def _(q):
        pl.semaphore_signal(barrier, inc=1, device_id=at_z(q), device_id_type=MESH)

    @pl.loop(1, PLANE)
    def _(q):
        pl.semaphore_signal(barrier, inc=1, device_id=at_plane(lax.rem(me + q, PLANE)), device_id_type=MESH)

    fetch.wait()
    fetch_ids.wait()
    low = p_ref[...].astype(LOW)
    docs[0, 0:R, :] = low
    own[y] = low
    ids[0, :, 0:R] = jnp.broadcast_to(a_ref[...], (8, R))
    pl.semaphore_wait(barrier, Z + PLANE - 2)

    def right(s, to, row, c):
        return remote(docs.at[s, pl.ds(c * CR, CR)], docs.at[to, pl.ds(row + c * CR, CR)],
                      zr_send.at[s, c], zr_recv.at[to, c], at_z(1))

    def left(s, row, to, c):
        return remote(docs.at[s, pl.ds(row + c * CR, CR)], docs.at[to, pl.ds(R + c * CR, CR)],
                      zl_send.at[s, c], zl_recv.at[to, c], at_z(-1))

    for c in range(CHUNKS):
        right(0, 1, 0, c).start()
        left(0, 0, 1, c).start()
    id_copies = []
    for q in range(1, Z):
        pair, half = (q % NP, int(q == NP)) if q <= NP else (Z - q, 1)
        id_copies.append(remote(
            ids.at[0, :, pl.ds(0, R)], ids.at[pair, :, pl.ds(half * R, R)],
            id_send.at[q], id_recv.at[q], at_z(q)))
        id_copies[-1].start()
    own_copies = []
    for q in range(1, Y):
        own_copies.append(remote(docs.at[0, pl.ds(0, R)], own.at[y], own_send.at[q], own_recv.at[q], at_y(q)))
        own_copies[-1].start()
    acc[...] = jnp.zeros_like(acc)
    sums[...] = jnp.zeros_like(sums)

    def partial(rows, unit, out, into):
        n = rows.shape[0]
        for v in range(Y):
            g = lax.dot_general(own[v], rows, NT, preferred_element_type=F32)
            out[:, v * SUB:(v + 1) * SUB, :] = g.reshape(B, SUB, n).astype(out.dtype)
        for q in range(1, B):
            to = lax.rem(b + q, B)
            remote(out.at[to], into.at[q - 1], rs_send.at[unit], rs_recv.at[unit], (doc, to)).start()

    def place(rows, a, column, unit):
        n = rows.shape[0]
        a = jnp.broadcast_to(a, (16, n))
        sub = iota((16, n), 0)
        lane = iota((16, n), 1)
        owner = jnp.where(sub < Y, lax.rem(y + sub, Y) * Z + z, -1)
        match = ((a & (GROUP - 1)) // PART) == owner
        local = (a // GROUP) * PART + (a & (PART - 1))
        earlier = (iota((n, n), 0) < iota((n, n), 1)) & (iota((n, n), 0) // R == iota((n, n), 1) // R)
        before = jnp.dot(match.astype(F32).astype(LOW), earlier.astype(F32).astype(LOW), preferred_element_type=F32)
        slot = jnp.where(match, before + CAP * (lane // R).astype(F32), -1.0)
        number = sub.astype(F32)
        pick = jnp.concatenate(
            [(number == slot[q:q + 1]).astype(F32).astype(LOW) for q in range(1, Y)], axis=0)
        home = (column // GROUP) * PART + (column & (PART - 1))
        home = (home == iota((n, 128), 1)).astype(F32).astype(LOW)
        picked = jnp.dot(pick, rows, preferred_element_type=F32).astype(LOW)
        where = jnp.dot(pick, home, preferred_element_type=F32).astype(LOW)
        for q in range(1, Y):
            pay_out[unit, q - 1, :, 0:W] = picked[(q - 1) * 16:q * 16]
            pay_out[unit, q - 1, :, W:W + 128] = where[(q - 1) * 16:q * 16]
            remote(pay_out.at[unit, q - 1], pay_in.at[unit, q - 1], pay_send.at[unit], pay_recv.at[unit], at_y(q)).start()
        row = jnp.where(match[0:1], local[0:1], -1)
        hot = (iota((OWN, n), 0) == row).astype(F32).astype(LOW)
        sums[...] += jnp.dot(hot, rows, preferred_element_type=F32)

    def add_placed(unit):
        wait_bytes(pay_in.at[unit], pay_recv.at[unit])
        for q in range(1, Y):
            d = lax.dot_general(pay_in[unit, q - 1, :, W:W + 128], pay_in[unit, q - 1, :, 0:W],
                                (((0,), (0,)), ((), ())), preferred_element_type=F32)
            sums[...] += d[0:OWN]

    def fold(out, into, column, first, count):
        h = out[b].astype(F32)
        for i in range(B - 1):
            h += into[i].astype(F32)
        hi = h.astype(LOW)
        lo = (h - hi.astype(F32)).astype(LOW)
        both = jnp.concatenate([hi, lo], axis=0)
        n = h.shape[1]
        for g in range(first, first + count):
            hot = jnp.concatenate(
                [(column == iota((n, 128), 1) + (g * GROUP + t * 128)).astype(F32).astype(LOW)
                 for t in range(GROUP // 128)], axis=1)
            d = jnp.dot(both, hot, preferred_element_type=F32)
            acc[:, g * GROUP:(g + 1) * GROUP] += d[0:NC] + d[NC:]

    @pl.loop(1, NP)
    def _(s):
        for c in range(CHUNKS):
            early = c < CHUNKS // 2
            right(0, s, 0, c).wait_recv()
            go = lambda: right(s, lax.rem(s + 1, NP), jnp.where(s == NP - 1, R, 0), c).start()
            go() if early else pl.when(s < NP - 1)(go)
            left(0, 0, s, c).wait_recv()
            go_left = lambda: left(s, R, lax.rem(s + 1, NP), c).start()
            pl.when(s < NP - 1)(go_left) if early else go_left()

            if c == 0:

                @pl.when(s == 2)
                def _():
                    for copy in id_copies:
                        copy.wait()
                    for q in range(1, Y):
                        own_copies[q - 1].wait_send()
                        from_y = lax.rem(y - q + Y, Y)
                        remote(own.at[0], own.at[from_y], own_send.at[q], own_recv.at[q], (doc, b)).wait_recv()

                    @pl.loop(0, NP)
                    def _(p):
                        col[p] = jnp.transpose(jnp.broadcast_to(ids[p, 0:1, :], (128, 2 * R)))

                pl.when(s >= 2)(lambda: partial(docs[s - 1], s - 1, part.at[s - 2], got.at[s - 2]))

            if c == 1:
                pl.when(s >= 2)(lambda: place(docs[s - 1], ids[s - 1, 0:1, :], col[s - 1], s - 1))

                @pl.when(s == 2)
                def _():
                    place(docs[0, 0:R, :], ids[0, 0:1, 0:R], col[0, 0:R, :], 0)
                    partial(docs[0, 0:R, :], 0, part0, got0)

            if c >= 2:

                @pl.when(s >= 3)
                def _():
                    p = s - 2
                    if c == 2:
                        wait_bytes(got.at[p - 1], rs_recv.at[p])
                    half = B // 2
                    fold(part.at[p - 1], got.at[p - 1], col[p], (c - 2) * half, half)
                    if c == 3:
                        add_placed(p)

    place(docs[NP - 1], ids[NP - 1, 0:1, :], col[NP - 1], NP - 1)
    partial(docs[NP - 1], NP - 1, part_pen, got_pen)
    wait_bytes(got0, rs_recv.at[0])
    fold(part0, got0, col[0, 0:R, :], 0, B)
    add_placed(0)
    for c in range(CHUNKS // 2):
        right(0, 0, R, c).wait_recv()
        left(0, 0, 0, c + CHUNKS // 2).wait_recv()
    place(docs[0, R:2 * R, :], ids[0, 0:1, R:2 * R], col[0, R:2 * R, :], LAST)
    partial(docs[0, R:2 * R, :], LAST, part_last, got_last)
    wait_bytes(got.at[NP - 3], rs_recv.at[NP - 2])
    fold(part.at[NP - 3], got.at[NP - 3], col[NP - 2], 0, B)
    add_placed(NP - 2)
    add_placed(NP - 1)
    add_placed(LAST)

    def slab_copy(to):
        return remote(sums.at[pl.ds(pl.multiple_of(to * PART, PART), PART)],
                      cent_raw.at[:, pl.ds(pl.multiple_of(b * W, W), W)], u_send, u_recv, (doc, to))

    square = jnp.sum(sums[...] * sums[...], axis=1, keepdims=True)
    square = jnp.broadcast_to(square, (OWN, 128))
    if OWN < 128:
        square = jnp.concatenate([square, jnp.zeros((128 - OWN, 128), F32)], axis=0)
    sq_out[...] = jnp.transpose(square)[0:1]

    @pl.loop(1, PLANE)
    def _(q):
        idx = lax.rem(me + q, PLANE)
        remote(sq_out, sq_in.at[PLANE - 1 - q], sq_send, sq_recv, at_plane(idx)).start()

    for q in range(1, B):
        slab_copy(lax.rem(b + q, B)).start()
    cent_raw[:, pl.ds(pl.multiple_of(b * W, W), W)] = sums[pl.ds(pl.multiple_of(b * PART, PART), PART), :]

    wait_bytes(got_pen, rs_recv.at[NP - 1])
    fold(part_pen, got_pen, col[NP - 1], 0, B)
    wait_bytes(got_last, rs_recv.at[LAST])
    fold(part_last, got_last, col[0, R:2 * R, :], 0, B)

    for g in range(B):
        fold_out[g] = acc[:, g * GROUP:(g + 1) * GROUP].astype(LOW)

    def fold_piece(idx):
        v, g = idx // B, lax.rem(idx, B)
        return fold_out.at[g, pl.ds(pl.multiple_of(v * SUB, SUB), SUB)], fold_in.at[me]

    @pl.loop(1, PLANE)
    def _(q):
        idx = lax.rem(me + q, PLANE)
        src, dst = fold_piece(idx)
        remote(src, dst, f_send, f_recv, at_plane(idx)).start()

    src, dst = fold_piece(me)
    pltpu.make_async_copy(src, dst, f_recv).start()

    wait_bytes(sq_in, sq_recv)
    sub = iota((8, 128), 0)
    lane = iota((8, 128), 1)
    table = jnp.zeros((8, 128), F32)
    for i in range(PLANE):
        row = sq_out[...] if i == PLANE - 1 else sq_in[i]
        v = lax.rem(me + i + 1, PLANE) // B
        table += jnp.where(sub == v, row, 0.0)
    inverse = lax.rsqrt(table + EPS)
    turned = pltpu.roll(inverse, lax.rem((z - b) * PART + 128, 128), 1)
    turned = jnp.where((lane >= z * PART) & (lane < (z + 1) * PART), turned, 0.0)
    nrm[Z - 1] = turned[0:Y]

    @pl.loop(1, Z)
    def _(q):
        remote(nrm.at[Z - 1], nrm.at[Z - 1 - q], nrm_send, nrm_recv, at_z(q)).start()

    ours = jnp.sum(jnp.where(sub == y, inverse, 0.0), axis=0, keepdims=True)
    colscale[...] = jnp.transpose(jnp.broadcast_to(ours, (128, 128)))
    scale = colscale[pl.ds(pl.multiple_of(b * PART, PART), PART), :]
    wait_bytes(cent_raw.at[:, pl.ds(0, (B - 1) * W)], u_recv)
    for t in range(B * W // 128):
        cent_ref[0, :, t * 128:(t + 1) * 128] = cent_raw[:, t * 128:(t + 1) * 128] * scale

    wait_bytes(fold_in, f_recv)
    raw = fold_in[0:B].astype(F32)
    for v in range(1, Y):
        raw += fold_in[v * B:(v + 1) * B].astype(F32)
    raw = raw.reshape(R, GROUP)
    wait_bytes(nrm.at[pl.ds(0, Z - 1)], nrm_recv)
    rows = nrm[0]
    for i in range(1, Z):
        rows += nrm[i]
    for v in range(Y):
        tile = raw[:, v * LANES:(v + 1) * LANES] * rows[v:v + 1, :]
        score_ref[v * LANES:(v + 1) * LANES, :] = jnp.transpose(tile)

    @pl.loop(0, NP)
    def _(s):
        for c in range(CHUNKS):
            early = c < CHUNKS // 2
            wait_right = lambda: right(s, s, 0, c).wait_send()
            wait_left = lambda: left(s, 0, s, c).wait_send()
            wait_right() if early else pl.when(s < NP - 1)(wait_right)
            pl.when(s < NP - 1)(wait_left) if early else wait_left()

    for p in range(NP - 2):
        wait_bytes(got.at[p], rs_send.at[p + 1])
    wait_bytes(got0, rs_send.at[0])
    wait_bytes(got_pen, rs_send.at[NP - 1])
    wait_bytes(got_last, rs_send.at[LAST])
    for u in range(NP + 1):
        wait_bytes(pay_in.at[u], pay_send.at[u])
    wait_bytes(fold_in.at[pl.ds(0, PLANE - 1)], f_send)
    wait_bytes(sq_in, sq_send)
    wait_bytes(nrm.at[pl.ds(0, Z - 1)], nrm_send)
    wait_bytes(cent_raw.at[:, pl.ds(0, (B - 1) * W)], u_send)


def program(mesh, Z, clusters):
    B = mesh.shape["bin"]
    Y = mesh.shape["doc"] // Z
    NP = Z // 2

    def shards(profiles, assign):
        R, W = profiles.shape
        group = clusters // B
        part = group // (Y * Z)
        own = part * B
        SUB = R // B
        NC = Y * SUB
        plane = Y * B
        dma = pltpu.SemaphoreType.DMA
        scratch = [
            pltpu.VMEM((R, W), F32),
            pltpu.VMEM((1, R), jnp.int32),
            pltpu.VMEM((NP, 2 * R, W), LOW),
            pltpu.VMEM((Y, R, W), LOW),
            pltpu.VMEM((NP, 8, 2 * R), jnp.int32),
            pltpu.VMEM((NP, 2 * R, 128), jnp.int32),
            pltpu.VMEM((NP - 2, B, NC, 2 * R), F32),
            pltpu.VMEM((NP - 2, B - 1, NC, 2 * R), F32),
            pltpu.VMEM((B, NC, R), F32),
            pltpu.VMEM((B - 1, NC, R), F32),
            pltpu.VMEM((B, NC, 2 * R), LOW),
            pltpu.VMEM((B - 1, NC, 2 * R), LOW),
            pltpu.VMEM((B, NC, R), LOW),
            pltpu.VMEM((B - 1, NC, R), LOW),
            pltpu.VMEM((NC, clusters), F32),
            pltpu.VMEM((own, W), F32),
            pltpu.VMEM((NP + 1, Y - 1, 16, W + 128), LOW),
            pltpu.VMEM((NP + 1, Y - 1, 16, W + 128), LOW),
            pltpu.VMEM((1, 128), F32),
            pltpu.VMEM((plane - 1, 1, 128), F32),
            pltpu.VMEM((Z, Y, 128), F32),
            pltpu.VMEM((B, NC, group), LOW),
            pltpu.VMEM((plane, SUB, group), LOW),
            pltpu.VMEM((part, B * W), F32),
            pltpu.VMEM((128, 128), F32),
            dma((2,)),
            *[dma((NP, CHUNKS))] * 4,
            *[dma((Z,))] * 2,
            *[dma((Y,))] * 2,
            *[dma((NP + 1,))] * 4,
            *[dma] * 8,
        ]
        return pl.pallas_call(
            functools.partial(kernel, Y, Z, B, clusters),
            out_shape=(
                jax.ShapeDtypeStruct((1, part, B * W), F32),
                jax.ShapeDtypeStruct((group, R), F32),
            ),
            in_specs=[pl.BlockSpec(memory_space=pltpu.HBM)] * 2,
            out_specs=(pl.BlockSpec(memory_space=pltpu.VMEM),) * 2,
            scratch_shapes=scratch,
            compiler_params=pltpu.CompilerParams(
                collective_id=0, has_side_effects=True, vmem_limit_bytes=48 * 2**20
            ),
        )(profiles, assign.reshape(1, -1))

    return jax.shard_map(
        shards,
        mesh=mesh,
        in_specs=(P("doc", "bin"), P("doc")),
        out_specs=(P("bin", "doc", None), P("bin", "doc")),
        check_vma=False,
    )


def solution(mesh):
    return program(mesh, DEPTH, 4096)
```

```python
import functools

import jax
import jax.numpy as jnp
from jax import lax
from jax.experimental import pallas as pl
from jax.experimental.pallas import tpu as pltpu
from jax.sharding import PartitionSpec as P

MESH = pl.DeviceIdType.MESH
EPS = 1e-06
DEPTH = 16
CHUNKS = 4
F32 = jnp.float32
LOW = jnp.bfloat16
NT = (((1,), (1,)), ((), ()))


def iota(shape, dim):
    return lax.broadcasted_iota(jnp.int32, shape, dim)


def kernel(
    Y, Z, B, K, p_hbm, a_hbm, cent_ref, score_ref,
    p_ref, a_ref, docs, own, ids, col, part, got, part0, got0, part_pen, got_pen, part_last, got_last,
    acc, sums, pay_out, pay_in, sq_out, sq_in, nrm, fold_out, fold_in, cent_raw, colscale, pick_last, where_last, hot_last, fold_hot,
    in_sem, zr_send, zr_recv, zl_send, zl_recv, id_send, id_recv, own_send, own_recv,
    rs_send, rs_recv, pay_send, pay_recv, sq_send, sq_recv, nrm_send, nrm_recv,
    f_send, f_recv, u_send, u_recv,
):
    R, W = p_ref.shape
    NP = Z // 2
    LAST = NP
    PLANE = Y * B
    GROUP = K // B
    PART = GROUP // (Y * Z)
    OWN = PART * B
    LANES = PART * Z
    CR = R // CHUNKS
    SUB = R // B
    NC = Y * SUB
    CAP = 8
    HALF = NP // 2
    doc, b = lax.axis_index("doc"), lax.axis_index("bin")
    y, z = doc // Z, doc & (Z - 1)
    me = y * B + b

    def at_z(q):
        return (y * Z + ((z + q) & (Z - 1)), b)

    def at_y(q):
        return (((y + q) & (Y - 1)) * Z + z, b)

    def at_plane(idx):
        return ((idx // B) * Z + z, idx & (B - 1))

    def remote(src, dst, send, recv, device):
        return pltpu.make_async_remote_copy(
            src_ref=src, dst_ref=dst, send_sem=send, recv_sem=recv, device_id=device, device_id_type=MESH
        )

    def wait_bytes(ref, sem):
        pltpu.make_async_copy(ref, ref, sem).wait()

    fetch = pltpu.make_async_copy(p_hbm, p_ref, in_sem.at[0])
    fetch.start()
    fetch_ids = pltpu.make_async_copy(a_hbm, a_ref, in_sem.at[1])
    fetch_ids.start()

    barrier = pltpu.get_barrier_semaphore()

    for q in range(1, HALF + 1):
        for way in (q, -q):
            pl.semaphore_signal(barrier, inc=1, device_id=at_z(way), device_id_type=MESH)

    @pl.loop(1, PLANE)
    def _(q):
        pl.semaphore_signal(barrier, inc=1, device_id=at_plane(((me + q) & (PLANE - 1))), device_id_type=MESH)

    fetch.wait()
    fetch_ids.wait()
    low = p_ref[...].astype(LOW)
    docs[0, 0:R, :] = low
    own[y] = low
    ids[0, :, 0:R] = a_ref[...]
    pl.semaphore_wait(barrier, 2 * HALF + PLANE - 1)

    def right(s, to, row, c):
        return remote(docs.at[s, pl.ds(c * CR, CR)], docs.at[to, pl.ds(row + c * CR, CR)],
                      zr_send.at[s, c], zr_recv.at[to, c], at_z(1))

    def left(s, row, to, c):
        return remote(docs.at[s, pl.ds(row + c * CR, CR)], docs.at[to, pl.ds(R + c * CR, CR)],
                      zl_send.at[s, c], zl_recv.at[to, c], at_z(-1))

    for c in range(CHUNKS):
        right(0, 1, 0, c).start()
        left(0, 0, 1, c).start()
    id_near, id_far = [], []
    for q in range(1, HALF + 1):
        for side, way in ((0, q), (1, -q)):
            k = 2 * q + side
            id_near.append(remote(ids.at[0, :, pl.ds(0, R)], ids.at[q, :, pl.ds(side * R, R)],
                                  id_send.at[k], id_recv.at[k], at_z(way)))
            if q < HALF or side:
                lanes = pl.ds(side * R, R)
                k += 2 * HALF
                id_far.append(remote(ids.at[q, :, lanes], ids.at[(q + HALF) % NP, :, lanes],
                                     id_send.at[k], id_recv.at[k], at_z(-HALF if side else HALF)))
    for copy in id_near:
        copy.start()
    def own_copy(q):
        return remote(docs.at[0, pl.ds(0, R)], own.at[y], own_send.at[q], own_recv.at[q], at_y(q))

    for q in range(1, Y):
        own_copy(q).start()
    acc[...] = jnp.zeros_like(acc)
    sums[...] = jnp.zeros_like(sums)

    def partial(rows, unit, out, into):
        n = rows.shape[0]
        for v in range(Y):
            g = lax.dot_general(own[v], rows, NT, preferred_element_type=F32)
            out[:, v * SUB:(v + 1) * SUB, :] = g.reshape(B, SUB, n).astype(out.dtype)
        for q in range(1, B):
            to = ((b + q) & (B - 1))
            remote(out.at[to], into.at[q - 1], rs_send.at[unit], rs_recv.at[unit], (doc, to)).start()

    def choose(a, column):
        n = a.shape[1]
        a = jnp.broadcast_to(a, (16, n))
        sub = iota((16, n), 0)
        lane = iota((16, n), 1)
        owner = jnp.where(sub < 2 * Y, lax.rem(y + sub // 2, Y) * Z + lax.rem(z + (sub & 1) * NP, Z), -1)
        match = ((a & (GROUP - 1)) // PART) == owner
        local = (a // GROUP) * PART + (a & (PART - 1))
        earlier = (iota((n, n), 0) < iota((n, n), 1)) & (iota((n, n), 0) // R == iota((n, n), 1) // R)
        before = jnp.dot(match.astype(F32).astype(LOW), earlier.astype(F32).astype(LOW), preferred_element_type=F32)
        slot = jnp.where(match, before + CAP * (lane // R).astype(F32), -1.0)
        number = sub.astype(F32)
        if n == R:
            picks = [(number == slot[q:q + 1]) | (number - CAP == slot[q + 1:q + 2]) & (number >= CAP)
                     for q in range(2, 2 * Y, 2)]
        else:
            picks = [number == slot[q:q + 1] for q in range(2, 2 * Y)]
        pick = jnp.concatenate([hit.astype(F32).astype(LOW) for hit in picks], axis=0)
        home = (column // GROUP) * PART + (column & (PART - 1))
        home += jnp.where((((column & (GROUP - 1)) // PART) & (Z - 1)) == z, 0, OWN)
        home = (home == iota((n, 128), 1)).astype(F32).astype(LOW)
        where = jnp.dot(pick, home, preferred_element_type=F32).astype(LOW)
        row = jnp.where(match[0:1], local[0:1], jnp.where(match[1:2], local[1:2] + OWN, -1))
        hot = (iota((2 * OWN, n), 0) == row).astype(F32).astype(LOW)
        return pick, where, hot

    def place(rows, choice, unit):
        pick, where, hot = choice
        picked = jnp.dot(pick, rows, preferred_element_type=F32).astype(LOW)
        tall = pick.shape[0] // (Y - 1)
        for q in range(1, Y):
            out, into = pay_out.at[unit, q - 1, pl.ds(0, tall)], pay_in.at[unit, q - 1, pl.ds(0, tall)]
            out[:, 0:W] = picked[(q - 1) * tall:q * tall]
            out[:, W:W + 128] = where[(q - 1) * tall:q * tall]
            remote(out, into, pay_send.at[unit], pay_recv.at[unit], at_y(q)).start()
        sums[...] += jnp.dot(hot, rows, preferred_element_type=F32)

    def add_placed(unit, tall=32):
        wait_bytes(pay_in.at[unit, :, pl.ds(0, tall)], pay_recv.at[unit])
        for q in range(1, Y):
            d = lax.dot_general(pay_in[unit, q - 1, 0:tall, W:W + 128], pay_in[unit, q - 1, 0:tall, 0:W],
                                (((0,), (0,)), ((), ())), preferred_element_type=F32)
            sums[...] += d[0:2 * OWN]

    def spread(column, g):
        return jnp.concatenate(
            [(column == iota((column.shape[0], 128), 1) + (g * GROUP + t * 128)).astype(F32).astype(LOW)
             for t in range(GROUP // 128)], axis=1)

    def ready(at, column):
        for g in range(B):
            fold_hot[g, at:at + column.shape[0], :] = spread(column, g)

    def finished(out, into):
        h = out[b].astype(F32)
        for i in range(B - 1):
            h += into[i].astype(F32)
        hi = h.astype(LOW)
        lo = (h - hi.astype(F32)).astype(LOW)
        return jnp.concatenate([hi, lo], axis=0)

    def fold(out, into, column, first, count, at=0):
        both = finished(out, into)
        n = both.shape[1]
        for g in range(first, first + count):
            hot = fold_hot[g, at:at + n, :] if column is None else spread(column, g)
            d = jnp.dot(both, hot, preferred_element_type=F32)
            acc[g] += d[0:NC] + d[NC:]

    @pl.loop(1, NP)
    def _(s):
        for c in range(CHUNKS):
            early = c < CHUNKS // 2
            right(0, s, 0, c).wait_recv()
            go = lambda: right(s, ((s + 1) & (NP - 1)), jnp.where(s == NP - 1, R, 0), c).start()
            go() if early else pl.when(s < NP - 1)(go)
            left(0, 0, s, c).wait_recv()
            go_left = lambda: left(s, R, ((s + 1) & (NP - 1)), c).start()
            pl.when(s < NP - 1)(go_left) if early else go_left()

            if c == 0:

                @pl.when(s == 1)
                def _():
                    for copy in id_near:
                        copy.wait()
                    for copy in id_far:
                        copy.start()

                @pl.when(s == 2)
                def _():
                    for copy in id_far:
                        copy.wait()
                    for q in range(1, Y):
                        own_copy(q).wait_send()
                        from_y = lax.rem(y - q + Y, Y)
                        remote(own.at[0], own.at[from_y], own_send.at[q], own_recv.at[q], (doc, b)).wait_recv()

                    @pl.loop(0, NP)
                    def _(p):
                        col[p] = jnp.transpose(jnp.broadcast_to(ids[p, 0:1, :], (128, 2 * R)))

                pl.when(s >= 2)(lambda: partial(docs[s - 1], s - 1, part.at[s - 2], got.at[s - 2]))

            if c == 1:
                pl.when(s >= 2)(lambda: place(docs[s - 1], choose(ids[s - 1], col[s - 1]), s - 1))

                @pl.when(s == 2)
                def _():
                    place(docs[0, 0:R, :], choose(ids[0, :, 0:R], col[0, 0:R, :]), 0)
                    partial(docs[0, 0:R, :], 0, part0, got0)

                @pl.when(s == 3)
                def _():
                    pick_last[...], where_last[...], hot_last[...] = choose(ids[0, :, R:2 * R], col[0, R:2 * R, :])
                    ready(4 * R, col[0, R:2 * R, :])

                pl.when(s == max(3, NP - 4))(lambda: ready(0, col[NP - 2]))
                pl.when(s == max(3, NP - 3))(lambda: ready(2 * R, col[NP - 1]))

                @pl.when(s == max(3, NP - 4))
                def _():
                    wait_bytes(got0, rs_recv.at[0])
                    fold(part0, got0, col[0, 0:R, :], 0, B)
                    add_placed(0, 16)

            if c >= 2:

                @pl.when(s >= 3)
                def _():
                    p = s - 2
                    if c == 2:
                        wait_bytes(got.at[p - 1], rs_recv.at[p])
                    half = B // 2
                    fold(part.at[p - 1], got.at[p - 1], col[p], (c - 2) * half, half)
                    if c == 3:
                        add_placed(p)

    partial(docs[NP - 1], NP - 1, part_pen, got_pen)
    place(docs[NP - 1], choose(ids[NP - 1], col[NP - 1]), NP - 1)
    for c in range(CHUNKS // 2):
        right(0, 0, R, c).wait_recv()
        left(0, 0, 0, c + CHUNKS // 2).wait_recv()
    place(docs[0, R:2 * R, :], (pick_last[...], where_last[...], hot_last[...]), LAST)
    partial(docs[0, R:2 * R, :], LAST, part_last, got_last)
    wait_bytes(got.at[NP - 3], rs_recv.at[NP - 2])
    fold(part.at[NP - 3], got.at[NP - 3], None, 0, B, 0)
    add_placed(NP - 2)
    add_placed(NP - 1)
    wait_bytes(got_pen, rs_recv.at[NP - 1])
    fold(part_pen, got_pen, None, 0, B, 2 * R)
    add_placed(LAST, 16)

    def slab_copy(to):
        return remote(sums.at[pl.ds(pl.multiple_of(to * PART, PART), PART)],
                      cent_raw.at[:, pl.ds(pl.multiple_of(b * W, W), W)], u_send, u_recv, (doc, to))

    square = jnp.sum(sums[...] * sums[...], axis=1, keepdims=True)
    square = jnp.broadcast_to(square, (2 * OWN, 128))
    if 2 * OWN < 128:
        square = jnp.concatenate([square, jnp.zeros((128 - 2 * OWN, 128), F32)], axis=0)
    sq_out[...] = jnp.transpose(square)[0:1]

    @pl.loop(1, PLANE)
    def _(q):
        idx = ((me + q) & (PLANE - 1))
        remote(sq_out, sq_in.at[PLANE - 1 - q], sq_send, sq_recv, at_plane(idx)).start()

    wait_bytes(got_last, rs_recv.at[LAST])
    both = finished(part_last, got_last)

    def fold_piece(v, g):
        return fold_out.at[g, pl.ds(pl.multiple_of(v * SUB, SUB), SUB)], fold_in.at[me]

    for i in range(B):
        g = (b + 1 + i) & (B - 1)
        d = jnp.dot(both, fold_hot[g, 4 * R:5 * R, :], preferred_element_type=F32)
        fold_out[g] = (acc[g] + d[0:NC] + d[NC:]).astype(LOW)
        for j in range(Y):
            v = (y + j) & (Y - 1)
            src, dst = fold_piece(v, g)
            if i == B - 1 and j == 0:
                pltpu.make_async_copy(src, dst, f_recv).start()
            else:
                remote(src, dst, f_send, f_recv, (v * Z + z, g)).start()

    wait_bytes(sq_in, sq_recv)
    sub = iota((8, 128), 0)
    lane = iota((8, 128), 1)
    table = jnp.zeros((8, 128), F32)
    for i in range(PLANE):
        row = sq_out[...] if i == PLANE - 1 else sq_in[i]
        v = ((me + i + 1) & (PLANE - 1)) // B
        table += jnp.where(sub == v, row, 0.0)
    inverse = lax.rsqrt(table + EPS)
    far = lax.rem(z + NP, Z)
    near = pltpu.roll(inverse, lax.rem((z - b) * PART + 128, 128), 1)
    turned = jnp.where((lane >= z * PART) & (lane < (z + 1) * PART), near, 0.0)
    beyond = pltpu.roll(inverse, lax.rem((far - b) * PART - OWN + 256, 128), 1)
    turned += jnp.where((lane >= far * PART) & (lane < (far + 1) * PART), beyond, 0.0)
    nrm[NP - 1] = turned[0:Y]
    reach = [q for q in range(1 - NP // 2, NP // 2 + 1) if q]
    for i, q in enumerate(reach):
        remote(nrm.at[NP - 1], nrm.at[i], nrm_send, nrm_recv, at_z(q)).start()

    for q in range(1, B):
        slab_copy(((b + q) & (B - 1))).start()
    cent_raw[:, pl.ds(pl.multiple_of(b * W, W), W)] = sums[pl.ds(pl.multiple_of(b * PART, PART), PART), :]


    ours = jnp.sum(jnp.where(sub == y, inverse, 0.0), axis=0, keepdims=True)
    colscale[...] = jnp.transpose(jnp.broadcast_to(ours, (128, 128)))
    scale = colscale[pl.ds(pl.multiple_of(b * PART, PART), PART), :]
    wait_bytes(cent_raw.at[:, pl.ds(0, (B - 1) * W)], u_recv)
    for t in range(B * W // 128):
        cent_ref[0, :, t * 128:(t + 1) * 128] = cent_raw[:, t * 128:(t + 1) * 128] * scale

    wait_bytes(fold_in, f_recv)
    raw = fold_in[0:B].astype(F32)
    for v in range(1, Y):
        raw += fold_in[v * B:(v + 1) * B].astype(F32)
    raw = raw.reshape(R, GROUP)
    wait_bytes(nrm.at[pl.ds(0, NP - 1)], nrm_recv)
    rows = nrm[0]
    for i in range(1, NP):
        rows += nrm[i]
    for v in range(Y):
        tile = raw[:, v * LANES:(v + 1) * LANES] * rows[v:v + 1, :]
        score_ref[v * LANES:(v + 1) * LANES, :] = jnp.transpose(tile)

    @pl.loop(0, NP)
    def _(s):
        for c in range(CHUNKS):
            early = c < CHUNKS // 2
            wait_right = lambda: right(s, s, 0, c).wait_send()
            wait_left = lambda: left(s, 0, s, c).wait_send()
            wait_right() if early else pl.when(s < NP - 1)(wait_right)
            pl.when(s < NP - 1)(wait_left) if early else wait_left()

    for p in range(NP - 2):
        wait_bytes(got.at[p], rs_send.at[p + 1])
    wait_bytes(got0, rs_send.at[0])
    wait_bytes(got_pen, rs_send.at[NP - 1])
    wait_bytes(got_last, rs_send.at[LAST])
    for u in range(NP + 1):
        wait_bytes(pay_in.at[u, :, pl.ds(0, 16 if u in (0, LAST) else 32)], pay_send.at[u])
    wait_bytes(fold_in.at[pl.ds(0, PLANE - 1)], f_send)
    wait_bytes(sq_in, sq_send)
    wait_bytes(nrm.at[pl.ds(0, NP - 1)], nrm_send)
    wait_bytes(cent_raw.at[:, pl.ds(0, (B - 1) * W)], u_send)


def program(mesh, Z, clusters):
    B = mesh.shape["bin"]
    Y = mesh.shape["doc"] // Z
    NP = Z // 2

    def shards(profiles, assign):
        R, W = profiles.shape
        group = clusters // B
        part = group // (Y * Z)
        own = part * B
        SUB = R // B
        NC = Y * SUB
        plane = Y * B
        dma = pltpu.SemaphoreType.DMA
        scratch = [
            pltpu.VMEM((R, W), F32),
            pltpu.VMEM((1, R), jnp.int32),
            pltpu.VMEM((NP, 2 * R, W), LOW),
            pltpu.VMEM((Y, R, W), LOW),
            pltpu.VMEM((NP, 1, 2 * R), jnp.int32),
            pltpu.VMEM((NP, 2 * R, 128), jnp.int32),
            pltpu.VMEM((NP - 2, B, NC, 2 * R), LOW),
            pltpu.VMEM((NP - 2, B - 1, NC, 2 * R), LOW),
            pltpu.VMEM((B, NC, R), LOW),
            pltpu.VMEM((B - 1, NC, R), LOW),
            pltpu.VMEM((B, NC, 2 * R), LOW),
            pltpu.VMEM((B - 1, NC, 2 * R), LOW),
            pltpu.VMEM((B, NC, R), LOW),
            pltpu.VMEM((B - 1, NC, R), LOW),
            pltpu.VMEM((B, NC, group), F32),
            pltpu.VMEM((2 * own, W), F32),
            pltpu.VMEM((NP + 1, Y - 1, 32, W + 128), LOW),
            pltpu.VMEM((NP + 1, Y - 1, 32, W + 128), LOW),
            pltpu.VMEM((1, 128), F32),
            pltpu.VMEM((plane - 1, 1, 128), F32),
            pltpu.VMEM((NP, Y, 128), F32),
            pltpu.VMEM((B, NC, group), LOW),
            pltpu.VMEM((plane, SUB, group), LOW),
            pltpu.VMEM((part, B * W), F32),
            pltpu.VMEM((128, 128), F32),
            pltpu.VMEM(((Y - 1) * 16, R), LOW),
            pltpu.VMEM(((Y - 1) * 16, 128), LOW),
            pltpu.VMEM((2 * own, R), LOW),
            pltpu.VMEM((B, 5 * R, group), LOW),
            dma((2,)),
            *[dma((NP, CHUNKS))] * 4,
            *[dma((Z + 2,))] * 2,
            *[dma((Y,))] * 2,
            *[dma((NP + 1,))] * 4,
            *[dma] * 8,
        ]
        return pl.pallas_call(
            functools.partial(kernel, Y, Z, B, clusters),
            out_shape=(
                jax.ShapeDtypeStruct((1, part, B * W), F32),
                jax.ShapeDtypeStruct((group, R), F32),
            ),
            in_specs=[pl.BlockSpec(memory_space=pltpu.HBM)] * 2,
            out_specs=(pl.BlockSpec(memory_space=pltpu.VMEM),) * 2,
            scratch_shapes=scratch,
            compiler_params=pltpu.CompilerParams(
                collective_id=0, has_side_effects=True, vmem_limit_bytes=60 * 2**20
            ),
        )(profiles, assign.reshape(1, -1))

    return jax.shard_map(
        shards,
        mesh=mesh,
        in_specs=(P("doc", "bin"), P("doc")),
        out_specs=(P("bin", "doc", None), P("bin", "doc")),
        check_vma=False,
    )


def solution(mesh):
    return program(mesh, DEPTH, 4096)
```

```python
import functools

import jax
import jax.numpy as jnp
from jax import lax
from jax.experimental import pallas as pl
from jax.experimental.pallas import tpu as pltpu
from jax.sharding import PartitionSpec as P

MESH = pl.DeviceIdType.MESH
EPS = 1e-06
DEPTH = 16
CHUNKS = 4
F32 = jnp.float32
LOW = jnp.bfloat16
NT = (((1,), (1,)), ((), ()))


def iota(shape, dim):
    return lax.broadcasted_iota(jnp.int32, shape, dim)


def kernel(
    Y, Z, B, K, p_hbm, a_hbm, cent_ref, score_ref,
    p_ref, a_ref, docs, own, ids, col, part, got, part0, got0, part_pen, got_pen, part_last, got_last,
    acc, sums, pay_out, pay_in, sq_out, sq_in, nrm, fold_out, fold_in, cent_raw, colscale, pick_last, where_last, hot_last, fold_hot,
    in_sem, zr_send, zr_recv, zl_send, zl_recv, id_send, id_recv, own_send, own_recv,
    rs_send, rs_recv, pay_send, pay_recv, sq_send, sq_recv, nrm_send, nrm_recv,
    f_send, f_recv, u_send, u_recv,
):
    R, W = p_ref.shape
    NP = Z // 2
    LAST = NP
    PLANE = Y * B
    GROUP = K // B
    PART = GROUP // (Y * Z)
    OWN = PART * B
    LANES = PART * Z
    CR = R // CHUNKS
    SUB = R // B
    NC = Y * SUB
    CAP = 8
    HALF = NP // 2
    doc, b = lax.axis_index("doc"), lax.axis_index("bin")
    y, z = doc // Z, doc & (Z - 1)
    me = y * B + b

    def at_z(q):
        return (y * Z + ((z + q) & (Z - 1)), b)

    def at_y(q):
        return (((y + q) & (Y - 1)) * Z + z, b)

    def at_plane(idx):
        return ((idx // B) * Z + z, idx & (B - 1))

    def remote(src, dst, send, recv, device):
        return pltpu.make_async_remote_copy(
            src_ref=src, dst_ref=dst, send_sem=send, recv_sem=recv, device_id=device, device_id_type=MESH
        )

    def wait_bytes(ref, sem):
        pltpu.make_async_copy(ref, ref, sem).wait()

    fetch = pltpu.make_async_copy(p_hbm, p_ref, in_sem.at[0])
    fetch.start()
    fetch_ids = pltpu.make_async_copy(a_hbm, a_ref, in_sem.at[1])
    fetch_ids.start()

    barrier = pltpu.get_barrier_semaphore()

    for q in range(1, HALF + 1):
        for way in (q, -q):
            pl.semaphore_signal(barrier, inc=1, device_id=at_z(way), device_id_type=MESH)

    @pl.loop(1, PLANE)
    def _(q):
        pl.semaphore_signal(barrier, inc=1, device_id=at_plane(((me + q) & (PLANE - 1))), device_id_type=MESH)

    fetch.wait()
    fetch_ids.wait()
    low = p_ref[...].astype(LOW)
    docs[0, 0:R, :] = low
    own[y] = low
    ids[0, :, 0:R] = a_ref[...]
    pl.semaphore_wait(barrier, 2 * HALF + PLANE - 1)

    def right(s, to, row, c):
        return remote(docs.at[s, pl.ds(c * CR, CR)], docs.at[to, pl.ds(row + c * CR, CR)],
                      zr_send.at[s, c], zr_recv.at[to, c], at_z(1))

    def left(s, row, to, c):
        return remote(docs.at[s, pl.ds(row + c * CR, CR)], docs.at[to, pl.ds(R + c * CR, CR)],
                      zl_send.at[s, c], zl_recv.at[to, c], at_z(-1))

    for c in range(CHUNKS):
        right(0, 1, 0, c).start()
        left(0, 0, 1, c).start()
    id_near, id_far = [], []
    for q in range(1, HALF + 1):
        for side, way in ((0, q), (1, -q)):
            k = 2 * q + side
            id_near.append(remote(ids.at[0, :, pl.ds(0, R)], ids.at[q, :, pl.ds(side * R, R)],
                                  id_send.at[k], id_recv.at[k], at_z(way)))
            if q < HALF or side:
                lanes = pl.ds(side * R, R)
                k += 2 * HALF
                id_far.append(remote(ids.at[q, :, lanes], ids.at[(q + HALF) % NP, :, lanes],
                                     id_send.at[k], id_recv.at[k], at_z(-HALF if side else HALF)))
    for copy in id_near:
        copy.start()
    def own_copy(q):
        return remote(docs.at[0, pl.ds(0, R)], own.at[y], own_send.at[q], own_recv.at[q], at_y(q))

    for q in range(1, Y):
        own_copy(q).start()
    acc[...] = jnp.zeros_like(acc)
    sums[...] = jnp.zeros_like(sums)

    def partial(rows, unit, out, into):
        n = rows.shape[0]
        for v in range(Y):
            g = lax.dot_general(own[v], rows, NT, preferred_element_type=F32)
            out[:, v * SUB:(v + 1) * SUB, :] = g.reshape(B, SUB, n).astype(out.dtype)
        for q in range(1, B):
            to = ((b + q) & (B - 1))
            remote(out.at[to], into.at[q - 1], rs_send.at[unit], rs_recv.at[unit], (doc, to)).start()

    def choose(a, column):
        n = a.shape[1]
        a = jnp.broadcast_to(a, (16, n))
        sub = iota((16, n), 0)
        lane = iota((16, n), 1)
        owner = jnp.where(sub < 2 * Y, lax.rem(y + sub // 2, Y) * Z + lax.rem(z + (sub & 1) * NP, Z), -1)
        match = ((a & (GROUP - 1)) // PART) == owner
        local = (a // GROUP) * PART + (a & (PART - 1))
        earlier = (iota((n, n), 0) < iota((n, n), 1)) & (iota((n, n), 0) // R == iota((n, n), 1) // R)
        before = jnp.dot(match.astype(F32).astype(LOW), earlier.astype(F32).astype(LOW), preferred_element_type=F32)
        slot = jnp.where(match, before + CAP * (lane // R).astype(F32), -1.0)
        number = sub.astype(F32)
        if n == R:
            picks = [(number == slot[q:q + 1]) | (number - CAP == slot[q + 1:q + 2]) & (number >= CAP)
                     for q in range(2, 2 * Y, 2)]
        else:
            picks = [number == slot[q:q + 1] for q in range(2, 2 * Y)]
        pick = jnp.concatenate([hit.astype(F32).astype(LOW) for hit in picks], axis=0)
        home = (column // GROUP) * PART + (column & (PART - 1))
        home += jnp.where((((column & (GROUP - 1)) // PART) & (Z - 1)) == z, 0, OWN)
        home = (home == iota((n, 128), 1)).astype(F32).astype(LOW)
        where = jnp.dot(pick, home, preferred_element_type=F32).astype(LOW)
        row = jnp.where(match[0:1], local[0:1], jnp.where(match[1:2], local[1:2] + OWN, -1))
        hot = (iota((2 * OWN, n), 0) == row).astype(F32).astype(LOW)
        return pick, where, hot

    def place(rows, choice, unit):
        pick, where, hot = choice
        picked = jnp.dot(pick, rows, preferred_element_type=F32).astype(LOW)
        tall = pick.shape[0] // (Y - 1)
        for q in range(1, Y):
            out, into = pay_out.at[unit, q - 1, pl.ds(0, tall)], pay_in.at[unit, q - 1, pl.ds(0, tall)]
            out[:, 0:W] = picked[(q - 1) * tall:q * tall]
            out[:, W:W + 128] = where[(q - 1) * tall:q * tall]
            remote(out, into, pay_send.at[unit], pay_recv.at[unit], at_y(q)).start()
        sums[...] += jnp.dot(hot, rows, preferred_element_type=F32)

    def add_placed(unit, tall=32):
        wait_bytes(pay_in.at[unit, :, pl.ds(0, tall)], pay_recv.at[unit])
        for q in range(1, Y):
            d = lax.dot_general(pay_in[unit, q - 1, 0:tall, W:W + 128], pay_in[unit, q - 1, 0:tall, 0:W],
                                (((0,), (0,)), ((), ())), preferred_element_type=F32)
            sums[...] += d[0:2 * OWN]

    def spread(column, g):
        return jnp.concatenate(
            [(column == iota((column.shape[0], 128), 1) + (g * GROUP + t * 128)).astype(F32).astype(LOW)
             for t in range(GROUP // 128)], axis=1)

    def ready(at, column):
        for g in range(B):
            fold_hot[g, at:at + column.shape[0], :] = spread(column, g)

    def finished(out, into):
        h = out[b].astype(F32)
        for i in range(B - 1):
            h += into[i].astype(F32)
        hi = h.astype(LOW)
        lo = (h - hi.astype(F32)).astype(LOW)
        return jnp.concatenate([hi, lo], axis=0)

    def fold(out, into, column, first, count, at=0):
        both = finished(out, into)
        n = both.shape[1]
        for g in range(first, first + count):
            hot = fold_hot[g, at:at + n, :] if column is None else spread(column, g)
            d = jnp.dot(both, hot, preferred_element_type=F32)
            acc[g] += d[0:NC] + d[NC:]

    def column(p):
        return jnp.transpose(jnp.broadcast_to(ids[p], (128, 2 * R)))

    @pl.loop(1, NP)
    def _(s):
        for c in range(CHUNKS):
            early = c < CHUNKS // 2
            right(0, s, 0, c).wait_recv()
            go = lambda: right(s, ((s + 1) & (NP - 1)), jnp.where(s == NP - 1, R, 0), c).start()
            go() if early else pl.when(s < NP - 1)(go)
            left(0, 0, s, c).wait_recv()
            go_left = lambda: left(s, R, ((s + 1) & (NP - 1)), c).start()
            pl.when(s < NP - 1)(go_left) if early else go_left()

            if c == 0:

                @pl.when(s == 1)
                def _():
                    for copy in id_near:
                        copy.wait()
                    for copy in id_far:
                        copy.start()

                @pl.when(s == 2)
                def _():
                    for copy in id_far:
                        copy.wait()

                @pl.when(s >= 2)
                def _():
                    col[s - 1] = column(s - 1)
                    place(docs[s - 1], choose(ids[s - 1], col[s - 1]), s - 1)

                @pl.when(s == 3)
                def _():
                    place(docs[0, 0:R, :], choose(ids[0, :, 0:R], column(0)[0:R]), 0)

            if c == 1:

                @pl.when(s == 2)
                def _():
                    for q in range(1, Y):
                        own_copy(q).wait_send()
                        from_y = (y - q) & (Y - 1)
                        remote(own.at[0], own.at[from_y], own_send.at[q], own_recv.at[q], (doc, b)).wait_recv()

                pl.when(s >= 2)(lambda: partial(docs[s - 1], s - 1, part.at[s - 2], got.at[s - 2]))
                pl.when(s == 3)(lambda: partial(docs[0, 0:R, :], 0, part0, got0))
                pl.when(s == max(3, NP - 4))(lambda: ready(0, column(NP - 2)))
                pl.when(s == max(3, NP - 2))(lambda: ready(2 * R, column(NP - 1)))

                @pl.when(s == max(3, NP - 3))
                def _():
                    last = column(0)[R:2 * R]
                    pick_last[...], where_last[...], hot_last[...] = choose(ids[0, :, R:2 * R], last)
                    ready(4 * R, last)

            if c == 2:

                @pl.when(s == max(3, NP - 4))
                def _():
                    wait_bytes(got0, rs_recv.at[0])
                    fold(part0, got0, column(0)[0:R], 0, B)
                    add_placed(0, 16)

            if c >= 2:

                @pl.when(s >= 3)
                def _():
                    p = s - 2
                    if c == 2:
                        wait_bytes(got.at[p - 1], rs_recv.at[p])
                    half = B // 2
                    fold(part.at[p - 1], got.at[p - 1], col[p], (c - 2) * half, half)
                    if c == 3:
                        add_placed(p)

    partial(docs[NP - 1], NP - 1, part_pen, got_pen)
    place(docs[NP - 1], choose(ids[NP - 1], column(NP - 1)), NP - 1)
    for c in range(CHUNKS // 2):
        right(0, 0, R, c).wait_recv()
        left(0, 0, 0, c + CHUNKS // 2).wait_recv()
    place(docs[0, R:2 * R, :], (pick_last[...], where_last[...], hot_last[...]), LAST)
    partial(docs[0, R:2 * R, :], LAST, part_last, got_last)
    wait_bytes(got.at[NP - 3], rs_recv.at[NP - 2])
    fold(part.at[NP - 3], got.at[NP - 3], None, 0, B, 0)
    add_placed(NP - 2)
    add_placed(NP - 1)
    wait_bytes(got_pen, rs_recv.at[NP - 1])
    fold(part_pen, got_pen, None, 0, B, 2 * R)
    add_placed(LAST, 16)

    def slab_copy(to):
        return remote(sums.at[pl.ds(pl.multiple_of(to * PART, PART), PART)],
                      cent_raw.at[:, pl.ds(pl.multiple_of(b * W, W), W)], u_send, u_recv, (doc, to))

    square = jnp.sum(sums[...] * sums[...], axis=1, keepdims=True)
    square = jnp.broadcast_to(square, (2 * OWN, 128))
    if 2 * OWN < 128:
        square = jnp.concatenate([square, jnp.zeros((128 - 2 * OWN, 128), F32)], axis=0)
    sq_out[...] = jnp.transpose(square)[0:1]

    @pl.loop(1, PLANE)
    def _(q):
        idx = ((me + q) & (PLANE - 1))
        remote(sq_out, sq_in.at[PLANE - 1 - q], sq_send, sq_recv, at_plane(idx)).start()

    wait_bytes(got_last, rs_recv.at[LAST])
    both = finished(part_last, got_last)

    def fold_piece(v, g):
        return fold_out.at[g, pl.ds(pl.multiple_of(v * SUB, SUB), SUB)], fold_in.at[me]

    for i in range(B):
        g = (b + 1 + i) & (B - 1)
        d = jnp.dot(both, fold_hot[g, 4 * R:5 * R, :], preferred_element_type=F32)
        fold_out[g] = (acc[g] + d[0:NC] + d[NC:]).astype(LOW)
        for j in range(Y):
            v = (y + j) & (Y - 1)
            src, dst = fold_piece(v, g)
            if i == B - 1 and j == 0:
                pltpu.make_async_copy(src, dst, f_recv).start()
            else:
                remote(src, dst, f_send, f_recv, (v * Z + z, g)).start()

    wait_bytes(sq_in, sq_recv)
    sub = iota((8, 128), 0)
    lane = iota((8, 128), 1)
    table = jnp.zeros((8, 128), F32)
    for i in range(PLANE):
        row = sq_out[...] if i == PLANE - 1 else sq_in[i]
        v = ((me + i + 1) & (PLANE - 1)) // B
        table += jnp.where(sub == v, row, 0.0)
    inverse = lax.rsqrt(table + EPS)
    far = lax.rem(z + NP, Z)
    near = pltpu.roll(inverse, lax.rem((z - b) * PART + 128, 128), 1)
    turned = jnp.where((lane >= z * PART) & (lane < (z + 1) * PART), near, 0.0)
    beyond = pltpu.roll(inverse, lax.rem((far - b) * PART - OWN + 256, 128), 1)
    turned += jnp.where((lane >= far * PART) & (lane < (far + 1) * PART), beyond, 0.0)
    nrm[NP - 1] = turned[0:Y]
    reach = [q for q in range(1 - NP // 2, NP // 2 + 1) if q]
    for i, q in enumerate(reach):
        remote(nrm.at[NP - 1], nrm.at[i], nrm_send, nrm_recv, at_z(q)).start()

    for q in range(1, B):
        slab_copy(((b + q) & (B - 1))).start()
    cent_raw[:, pl.ds(pl.multiple_of(b * W, W), W)] = sums[pl.ds(pl.multiple_of(b * PART, PART), PART), :]


    ours = jnp.sum(jnp.where(sub == y, inverse, 0.0), axis=0, keepdims=True)
    colscale[...] = jnp.transpose(jnp.broadcast_to(ours, (128, 128)))
    scale = colscale[pl.ds(pl.multiple_of(b * PART, PART), PART), :]
    wait_bytes(cent_raw.at[:, pl.ds(0, (B - 1) * W)], u_recv)
    for t in range(B * W // 128):
        cent_ref[0, :, t * 128:(t + 1) * 128] = cent_raw[:, t * 128:(t + 1) * 128] * scale

    wait_bytes(fold_in, f_recv)
    raw = fold_in[0:B].astype(F32)
    for v in range(1, Y):
        raw += fold_in[v * B:(v + 1) * B].astype(F32)
    raw = raw.reshape(R, GROUP)
    wait_bytes(nrm.at[pl.ds(0, NP - 1)], nrm_recv)
    rows = nrm[0]
    for i in range(1, NP):
        rows += nrm[i]
    for v in range(Y):
        tile = raw[:, v * LANES:(v + 1) * LANES] * rows[v:v + 1, :]
        score_ref[v * LANES:(v + 1) * LANES, :] = jnp.transpose(tile)

    @pl.loop(0, NP)
    def _(s):
        for c in range(CHUNKS):
            early = c < CHUNKS // 2
            wait_right = lambda: right(s, s, 0, c).wait_send()
            wait_left = lambda: left(s, 0, s, c).wait_send()
            wait_right() if early else pl.when(s < NP - 1)(wait_right)
            pl.when(s < NP - 1)(wait_left) if early else wait_left()

    for p in range(NP - 2):
        wait_bytes(got.at[p], rs_send.at[p + 1])
    wait_bytes(got0, rs_send.at[0])
    wait_bytes(got_pen, rs_send.at[NP - 1])
    wait_bytes(got_last, rs_send.at[LAST])
    for u in range(NP + 1):
        wait_bytes(pay_in.at[u, :, pl.ds(0, 16 if u in (0, LAST) else 32)], pay_send.at[u])
    wait_bytes(fold_in.at[pl.ds(0, PLANE - 1)], f_send)
    wait_bytes(sq_in, sq_send)
    wait_bytes(nrm.at[pl.ds(0, NP - 1)], nrm_send)
    wait_bytes(cent_raw.at[:, pl.ds(0, (B - 1) * W)], u_send)


def program(mesh, Z, clusters):
    B = mesh.shape["bin"]
    Y = mesh.shape["doc"] // Z
    NP = Z // 2

    def shards(profiles, assign):
        R, W = profiles.shape
        group = clusters // B
        part = group // (Y * Z)
        own = part * B
        SUB = R // B
        NC = Y * SUB
        plane = Y * B
        dma = pltpu.SemaphoreType.DMA
        scratch = [
            pltpu.VMEM((R, W), F32),
            pltpu.VMEM((1, R), jnp.int32),
            pltpu.VMEM((NP, 2 * R, W), LOW),
            pltpu.VMEM((Y, R, W), LOW),
            pltpu.VMEM((NP, 1, 2 * R), jnp.int32),
            pltpu.VMEM((NP, 2 * R, 128), jnp.int32),
            pltpu.VMEM((NP - 2, B, NC, 2 * R), LOW),
            pltpu.VMEM((NP - 2, B - 1, NC, 2 * R), LOW),
            pltpu.VMEM((B, NC, R), LOW),
            pltpu.VMEM((B - 1, NC, R), LOW),
            pltpu.VMEM((B, NC, 2 * R), LOW),
            pltpu.VMEM((B - 1, NC, 2 * R), LOW),
            pltpu.VMEM((B, NC, R), LOW),
            pltpu.VMEM((B - 1, NC, R), LOW),
            pltpu.VMEM((B, NC, group), F32),
            pltpu.VMEM((2 * own, W), F32),
            pltpu.VMEM((NP + 1, Y - 1, 32, W + 128), LOW),
            pltpu.VMEM((NP + 1, Y - 1, 32, W + 128), LOW),
            pltpu.VMEM((1, 128), F32),
            pltpu.VMEM((plane - 1, 1, 128), F32),
            pltpu.VMEM((NP, Y, 128), F32),
            pltpu.VMEM((B, NC, group), LOW),
            pltpu.VMEM((plane, SUB, group), LOW),
            pltpu.VMEM((part, B * W), F32),
            pltpu.VMEM((128, 128), F32),
            pltpu.VMEM(((Y - 1) * 16, R), LOW),
            pltpu.VMEM(((Y - 1) * 16, 128), LOW),
            pltpu.VMEM((2 * own, R), LOW),
            pltpu.VMEM((B, 5 * R, group), LOW),
            dma((2,)),
            *[dma((NP, CHUNKS))] * 4,
            *[dma((Z + 2,))] * 2,
            *[dma((Y,))] * 2,
            *[dma((NP + 1,))] * 4,
            *[dma] * 8,
        ]
        return pl.pallas_call(
            functools.partial(kernel, Y, Z, B, clusters),
            out_shape=(
                pltpu.VMEM((1, part, B * W), F32),
                pltpu.VMEM((group, R), F32),
            ),
            in_specs=[pl.BlockSpec(memory_space=pltpu.HBM)] * 2,
            out_specs=(pl.BlockSpec(memory_space=pltpu.VMEM),) * 2,
            scratch_shapes=scratch,
            compiler_params=pltpu.CompilerParams(
                collective_id=0, has_side_effects=True, vmem_limit_bytes=60 * 2**20
            ),
        )(profiles, assign.reshape(1, -1))

    return jax.shard_map(
        shards,
        mesh=mesh,
        in_specs=(P("doc", "bin"), P("doc")),
        out_specs=(P("bin", "doc", None), P("bin", "doc")),
        check_vma=False,
    )


def solution(mesh):
    return program(mesh, DEPTH, 4096)
```

```python
import functools

import jax
import jax.numpy as jnp
from jax import lax
from jax.experimental import pallas as pl
from jax.experimental.pallas import tpu as pltpu
from jax.sharding import PartitionSpec as P

MESH = pl.DeviceIdType.MESH
EPS = 1e-06
DEPTH = 16
CHUNKS = 4
F32 = jnp.float32
LOW = jnp.bfloat16
NT = (((1,), (1,)), ((), ()))


def iota(shape, dim):
    return lax.broadcasted_iota(jnp.int32, shape, dim)


def kernel(
    Y, Z, B, K, p_hbm, a_hbm, cent_ref, score_ref,
    p_ref, a_ref, docs, own, ids, col, part, got, part0, got0, part_pen, got_pen, part_last, got_last,
    acc, sums, pay_out, pay_in, sq_out, sq_in, nrm, fold_out, fold_in, cent_raw, colscale, pick_last, where_last, hot_last, fold_hot,
    in_sem, zr_send, zr_recv, zl_send, zl_recv, id_send, id_recv, own_send, own_recv,
    rs_send, rs_recv, pay_send, pay_recv, sq_send, sq_recv, nrm_send, nrm_recv,
    f_send, f_recv, u_send, u_recv,
):
    R, W = p_ref.shape
    NP = Z // 2
    LAST = NP
    PLANE = Y * B
    GROUP = K // B
    PART = GROUP // (Y * Z)
    OWN = PART * B
    LANES = PART * Z
    CR = R // CHUNKS
    SUB = R // B
    NC = Y * SUB
    CAP = 8
    HALF = NP // 2
    doc, b = lax.axis_index("doc"), lax.axis_index("bin")
    y, z = doc // Z, doc & (Z - 1)
    me = y * B + b

    def at_z(q):
        return (y * Z + ((z + q) & (Z - 1)), b)

    def at_y(q):
        return (((y + q) & (Y - 1)) * Z + z, b)

    def at_plane(idx):
        return ((idx // B) * Z + z, idx & (B - 1))

    def remote(src, dst, send, recv, device):
        return pltpu.make_async_remote_copy(
            src_ref=src, dst_ref=dst, send_sem=send, recv_sem=recv, device_id=device, device_id_type=MESH
        )

    def wait_bytes(ref, sem):
        pltpu.make_async_copy(ref, ref, sem).wait()

    fetch = pltpu.make_async_copy(p_hbm, p_ref, in_sem.at[0])
    fetch.start()
    fetch_ids = pltpu.make_async_copy(a_hbm, a_ref, in_sem.at[1])
    fetch_ids.start()

    barrier = pltpu.get_barrier_semaphore()

    for q in range(1, HALF + 1):
        for way in (q, -q):
            pl.semaphore_signal(barrier, inc=1, device_id=at_z(way), device_id_type=MESH)

    @pl.loop(1, PLANE)
    def _(q):
        pl.semaphore_signal(barrier, inc=1, device_id=at_plane(((me + q) & (PLANE - 1))), device_id_type=MESH)

    fetch.wait()
    fetch_ids.wait()
    low = p_ref[...].astype(LOW)
    docs[0, 0:R, :] = low
    own[y] = low
    ids[0, :, 0:R] = a_ref[...]
    pl.semaphore_wait(barrier, 2 * HALF + PLANE - 1)

    def right(s, to, row, c):
        return remote(docs.at[s, pl.ds(c * CR, CR)], docs.at[to, pl.ds(row + c * CR, CR)],
                      zr_send.at[s, c], zr_recv.at[to, c], at_z(1))

    def left(s, row, to, c):
        return remote(docs.at[s, pl.ds(row + c * CR, CR)], docs.at[to, pl.ds(R + c * CR, CR)],
                      zl_send.at[s, c], zl_recv.at[to, c], at_z(-1))

    for c in range(CHUNKS):
        right(0, 1, 0, c).start()
        left(0, 0, 1, c).start()
    id_near, id_far = [], []
    for q in range(1, HALF + 1):
        for side, way in ((0, q), (1, -q)):
            k = 2 * q + side
            id_near.append(remote(ids.at[0, :, pl.ds(0, R)], ids.at[q, :, pl.ds(side * R, R)],
                                  id_send.at[k], id_recv.at[k], at_z(way)))
            if q < HALF or side:
                lanes = pl.ds(side * R, R)
                k += 2 * HALF
                id_far.append(remote(ids.at[q, :, lanes], ids.at[(q + HALF) % NP, :, lanes],
                                     id_send.at[k], id_recv.at[k], at_z(-HALF if side else HALF)))
    for copy in id_near:
        copy.start()
    def own_copy(q):
        return remote(docs.at[0, pl.ds(0, R)], own.at[y], own_send.at[q], own_recv.at[q], at_y(q))

    for q in range(1, Y):
        own_copy(q).start()
    acc[...] = jnp.zeros_like(acc)
    sums[...] = jnp.zeros_like(sums)

    def partial(rows, unit, out, into):
        n = rows.shape[0]
        for v in range(Y):
            g = lax.dot_general(own[v], rows, NT, preferred_element_type=F32)
            out[:, v * SUB:(v + 1) * SUB, :] = g.reshape(B, SUB, n).astype(out.dtype)
        for q in range(1, B):
            to = ((b + q) & (B - 1))
            remote(out.at[to], into.at[q - 1], rs_send.at[unit], rs_recv.at[unit], (doc, to)).start()

    def choose(a, column):
        n = a.shape[1]
        a = jnp.broadcast_to(a, (16, n))
        sub = iota((16, n), 0)
        lane = iota((16, n), 1)
        owner = jnp.where(sub < 2 * Y, lax.rem(y + sub // 2, Y) * Z + lax.rem(z + (sub & 1) * NP, Z), -1)
        match = ((a & (GROUP - 1)) // PART) == owner
        local = (a // GROUP) * PART + (a & (PART - 1))
        earlier = (iota((n, n), 0) < iota((n, n), 1)) & (iota((n, n), 0) // R == iota((n, n), 1) // R)
        before = jnp.dot(match.astype(F32).astype(LOW), earlier.astype(F32).astype(LOW), preferred_element_type=F32)
        slot = jnp.where(match, before + CAP * (lane // R).astype(F32), -1.0)
        number = sub.astype(F32)
        if n == R:
            picks = [(number == slot[q:q + 1]) | (number - CAP == slot[q + 1:q + 2]) & (number >= CAP)
                     for q in range(2, 2 * Y, 2)]
        else:
            picks = [number == slot[q:q + 1] for q in range(2, 2 * Y)]
        pick = jnp.concatenate([hit.astype(F32).astype(LOW) for hit in picks], axis=0)
        home = (column // GROUP) * PART + (column & (PART - 1))
        home += jnp.where((((column & (GROUP - 1)) // PART) & (Z - 1)) == z, 0, OWN)
        home = (home == iota((n, 128), 1)).astype(F32).astype(LOW)
        where = jnp.dot(pick, home, preferred_element_type=F32).astype(LOW)
        row = jnp.where(match[0:1], local[0:1], jnp.where(match[1:2], local[1:2] + OWN, -1))
        hot = (iota((2 * OWN, n), 0) == row).astype(F32).astype(LOW)
        return pick, where, hot

    def place(rows, choice, unit):
        pick, where, hot = choice
        picked = jnp.dot(pick, rows, preferred_element_type=F32).astype(LOW)
        tall = pick.shape[0] // (Y - 1)
        for q in range(1, Y):
            out, into = pay_out.at[unit, q - 1, pl.ds(0, tall)], pay_in.at[unit, q - 1, pl.ds(0, tall)]
            out[:, 0:W] = picked[(q - 1) * tall:q * tall]
            out[:, W:W + 128] = where[(q - 1) * tall:q * tall]
            remote(out, into, pay_send.at[unit], pay_recv.at[unit], at_y(q)).start()
        sums[...] += jnp.dot(hot, rows, preferred_element_type=F32)

    def add_placed(unit, tall=32):
        wait_bytes(pay_in.at[unit, :, pl.ds(0, tall)], pay_recv.at[unit])
        for q in range(1, Y):
            d = lax.dot_general(pay_in[unit, q - 1, 0:tall, W:W + 128], pay_in[unit, q - 1, 0:tall, 0:W],
                                (((0,), (0,)), ((), ())), preferred_element_type=F32)
            sums[...] += d[0:2 * OWN]

    def spread(column, g):
        return jnp.concatenate(
            [(column == iota((column.shape[0], 128), 1) + (g * GROUP + t * 128)).astype(F32).astype(LOW)
             for t in range(GROUP // 128)], axis=1)

    def ready(at, column):
        for g in range(B):
            fold_hot[g, at:at + column.shape[0], :] = spread(column, g)

    def finished(out, into):
        h = out[b].astype(F32)
        for i in range(B - 1):
            h += into[i].astype(F32)
        hi = h.astype(LOW)
        lo = (h - hi.astype(F32)).astype(LOW)
        return jnp.concatenate([hi, lo], axis=0)

    def fold(out, into, column, first, count, at=0):
        both = finished(out, into)
        n = both.shape[1]
        for g in range(first, first + count):
            hot = fold_hot[g, at:at + n, :] if column is None else spread(column, g)
            d = jnp.dot(both, hot, preferred_element_type=F32)
            acc[g] += d[0:NC] + d[NC:]

    def column(p):
        return jnp.transpose(jnp.broadcast_to(ids[p], (128, 2 * R)))

    @pl.loop(1, NP)
    def _(s):
        for c in range(CHUNKS):
            early = c < CHUNKS // 2
            right(0, s, 0, c).wait_recv()
            go = lambda: right(s, ((s + 1) & (NP - 1)), jnp.where(s == NP - 1, R, 0), c).start()
            go() if early else pl.when(s < NP - 1)(go)
            left(0, 0, s, c).wait_recv()
            go_left = lambda: left(s, R, ((s + 1) & (NP - 1)), c).start()
            pl.when(s < NP - 1)(go_left) if early else go_left()

            if c == 0:

                @pl.when(s == 1)
                def _():
                    for copy in id_near:
                        copy.wait()
                    for copy in id_far:
                        copy.start()

                @pl.when(s == 2)
                def _():
                    for copy in id_far:
                        copy.wait()

                @pl.when(s >= 2)
                def _():
                    col[s - 1] = column(s - 1)
                    place(docs[s - 1], choose(ids[s - 1], col[s - 1]), s - 1)

                @pl.when(s == 3)
                def _():
                    place(docs[0, 0:R, :], choose(ids[0, :, 0:R], column(0)[0:R]), 0)

            if c == 1:

                @pl.when(s == 2)
                def _():
                    for q in range(1, Y):
                        own_copy(q).wait_send()
                        from_y = (y - q) & (Y - 1)
                        remote(own.at[0], own.at[from_y], own_send.at[q], own_recv.at[q], (doc, b)).wait_recv()

                pl.when(s >= 2)(lambda: partial(docs[s - 1], s - 1, part.at[s - 2], got.at[s - 2]))
                pl.when(s == 3)(lambda: partial(docs[0, 0:R, :], 0, part0, got0))
                pl.when(s == max(3, NP - 4))(lambda: ready(0, column(NP - 2)))
                pl.when(s == max(3, NP - 2))(lambda: ready(2 * R, column(NP - 1)))

                @pl.when(s == max(3, NP - 3))
                def _():
                    last = column(0)[R:2 * R]
                    pick_last[...], where_last[...], hot_last[...] = choose(ids[0, :, R:2 * R], last)
                    ready(4 * R, last)

            if c == 2:

                @pl.when(s == max(3, NP - 4))
                def _():
                    wait_bytes(got0, rs_recv.at[0])
                    fold(part0, got0, column(0)[0:R], 0, B)
                    add_placed(0, 16)

            if c >= 2:

                @pl.when(s >= 3)
                def _():
                    p = s - 2
                    if c == 2:
                        wait_bytes(got.at[p - 1], rs_recv.at[p])
                    half = B // 2
                    fold(part.at[p - 1], got.at[p - 1], col[p], (c - 2) * half, half)
                    if c == 3:
                        add_placed(p)

    partial(docs[NP - 1], NP - 1, part_pen, got_pen)
    place(docs[NP - 1], choose(ids[NP - 1], column(NP - 1)), NP - 1)
    for c in range(CHUNKS // 2):
        right(0, 0, R, c).wait_recv()
        left(0, 0, 0, c + CHUNKS // 2).wait_recv()
    place(docs[0, R:2 * R, :], (pick_last[...], where_last[...], hot_last[...]), LAST)
    partial(docs[0, R:2 * R, :], LAST, part_last, got_last)
    wait_bytes(got.at[NP - 3], rs_recv.at[NP - 2])
    fold(part.at[NP - 3], got.at[NP - 3], None, 0, B, 0)
    add_placed(NP - 2)
    add_placed(NP - 1)
    wait_bytes(got_pen, rs_recv.at[NP - 1])
    fold(part_pen, got_pen, None, 0, B, 2 * R)
    add_placed(LAST, 16)

    def slab_copy(to):
        return remote(sums.at[pl.ds(pl.multiple_of(to * PART, PART), PART)],
                      cent_raw.at[:, pl.ds(pl.multiple_of(b * W, W), W)], u_send, u_recv, (doc, to))

    square = jnp.sum(sums[...] * sums[...], axis=1, keepdims=True)
    square = jnp.broadcast_to(square, (2 * OWN, 128))
    if 2 * OWN < 128:
        square = jnp.concatenate([square, jnp.zeros((128 - 2 * OWN, 128), F32)], axis=0)
    sq_out[...] = jnp.transpose(square)[0:1]

    @pl.loop(1, PLANE)
    def _(q):
        idx = ((me + q) & (PLANE - 1))
        remote(sq_out, sq_in.at[PLANE - 1 - q], sq_send, sq_recv, at_plane(idx)).start()

    wait_bytes(got_last, rs_recv.at[LAST])
    both = finished(part_last, got_last)

    def fold_piece(v, g):
        return fold_out.at[g, pl.ds(pl.multiple_of(v * SUB, SUB), SUB)], fold_in.at[me]

    for i in range(B):
        g = (b + 1 + i) & (B - 1)
        d = jnp.dot(both, fold_hot[g, 4 * R:5 * R, :], preferred_element_type=F32)
        fold_out[g] = (acc[g] + d[0:NC] + d[NC:]).astype(LOW)
        for j in range(Y):
            v = (y + j) & (Y - 1)
            src, dst = fold_piece(v, g)
            if i == B - 1 and j == 0:
                pltpu.make_async_copy(src, dst, f_recv).start()
            else:
                remote(src, dst, f_send, f_recv, (v * Z + z, g)).start()

    wait_bytes(sq_in, sq_recv)
    sub = iota((8, 128), 0)
    lane = iota((8, 128), 1)
    table = jnp.zeros((8, 128), F32)
    for i in range(PLANE):
        row = sq_out[...] if i == PLANE - 1 else sq_in[i]
        v = ((me + i + 1) & (PLANE - 1)) // B
        table += jnp.where(sub == v, row, 0.0)
    inverse = lax.rsqrt(table + EPS)
    far = lax.rem(z + NP, Z)
    near = pltpu.roll(inverse, lax.rem((z - b) * PART + 128, 128), 1)
    turned = jnp.where((lane >= z * PART) & (lane < (z + 1) * PART), near, 0.0)
    beyond = pltpu.roll(inverse, lax.rem((far - b) * PART - OWN + 256, 128), 1)
    turned += jnp.where((lane >= far * PART) & (lane < (far + 1) * PART), beyond, 0.0)
    nrm[NP - 1] = turned[0:Y]
    reach = [q for q in range(1 - NP // 2, NP // 2 + 1) if q]
    for i, q in enumerate(reach):
        remote(nrm.at[NP - 1], nrm.at[i], nrm_send, nrm_recv, at_z(q)).start()

    for q in range(1, B):
        slab_copy(((b + q) & (B - 1))).start()
    cent_raw[:, pl.ds(pl.multiple_of(b * W, W), W)] = sums[pl.ds(pl.multiple_of(b * PART, PART), PART), :]


    @pl.loop(0, NP)
    def _(s):
        for c in range(CHUNKS):
            early = c < CHUNKS // 2
            wait_right = lambda: right(s, s, 0, c).wait_send()
            wait_left = lambda: left(s, 0, s, c).wait_send()
            wait_right() if early else pl.when(s < NP - 1)(wait_right)
            pl.when(s < NP - 1)(wait_left) if early else wait_left()

    for p in range(NP - 2):
        wait_bytes(got.at[p], rs_send.at[p + 1])
    wait_bytes(got0, rs_send.at[0])
    wait_bytes(got_pen, rs_send.at[NP - 1])
    wait_bytes(got_last, rs_send.at[LAST])
    for u in range(NP + 1):
        wait_bytes(pay_in.at[u, :, pl.ds(0, 16 if u in (0, LAST) else 32)], pay_send.at[u])

    ours = jnp.sum(jnp.where(sub == y, inverse, 0.0), axis=0, keepdims=True)
    colscale[...] = jnp.transpose(jnp.broadcast_to(ours, (128, 128)))
    scale = colscale[pl.ds(pl.multiple_of(b * PART, PART), PART), :]
    wait_bytes(cent_raw.at[:, pl.ds(0, (B - 1) * W)], u_recv)
    for t in range(B * W // 128):
        cent_ref[0, :, t * 128:(t + 1) * 128] = cent_raw[:, t * 128:(t + 1) * 128] * scale

    wait_bytes(fold_in, f_recv)
    raw = fold_in[0:B].astype(F32)
    for v in range(1, Y):
        raw += fold_in[v * B:(v + 1) * B].astype(F32)
    raw = raw.reshape(R, GROUP)
    wait_bytes(nrm.at[pl.ds(0, NP - 1)], nrm_recv)
    rows = nrm[0]
    for i in range(1, NP):
        rows += nrm[i]
    for v in range(Y):
        tile = raw[:, v * LANES:(v + 1) * LANES] * rows[v:v + 1, :]
        score_ref[v * LANES:(v + 1) * LANES, :] = jnp.transpose(tile)

    wait_bytes(fold_in.at[pl.ds(0, PLANE - 1)], f_send)
    wait_bytes(sq_in, sq_send)
    wait_bytes(nrm.at[pl.ds(0, NP - 1)], nrm_send)
    wait_bytes(cent_raw.at[:, pl.ds(0, (B - 1) * W)], u_send)


def program(mesh, Z, clusters):
    B = mesh.shape["bin"]
    Y = mesh.shape["doc"] // Z
    NP = Z // 2

    def shards(profiles, assign):
        R, W = profiles.shape
        group = clusters // B
        part = group // (Y * Z)
        own = part * B
        SUB = R // B
        NC = Y * SUB
        plane = Y * B
        dma = pltpu.SemaphoreType.DMA
        scratch = [
            pltpu.VMEM((R, W), F32),
            pltpu.VMEM((1, R), jnp.int32),
            pltpu.VMEM((NP, 2 * R, W), LOW),
            pltpu.VMEM((Y, R, W), LOW),
            pltpu.VMEM((NP, 1, 2 * R), jnp.int32),
            pltpu.VMEM((NP, 2 * R, 128), jnp.int32),
            pltpu.VMEM((NP - 2, B, NC, 2 * R), LOW),
            pltpu.VMEM((NP - 2, B - 1, NC, 2 * R), LOW),
            pltpu.VMEM((B, NC, R), LOW),
            pltpu.VMEM((B - 1, NC, R), LOW),
            pltpu.VMEM((B, NC, 2 * R), LOW),
            pltpu.VMEM((B - 1, NC, 2 * R), LOW),
            pltpu.VMEM((B, NC, R), LOW),
            pltpu.VMEM((B - 1, NC, R), LOW),
            pltpu.VMEM((B, NC, group), F32),
            pltpu.VMEM((2 * own, W), F32),
            pltpu.VMEM((NP + 1, Y - 1, 32, W + 128), LOW),
            pltpu.VMEM((NP + 1, Y - 1, 32, W + 128), LOW),
            pltpu.VMEM((1, 128), F32),
            pltpu.VMEM((plane - 1, 1, 128), F32),
            pltpu.VMEM((NP, Y, 128), F32),
            pltpu.VMEM((B, NC, group), LOW),
            pltpu.VMEM((plane, SUB, group), LOW),
            pltpu.VMEM((part, B * W), F32),
            pltpu.VMEM((128, 128), F32),
            pltpu.VMEM(((Y - 1) * 16, R), LOW),
            pltpu.VMEM(((Y - 1) * 16, 128), LOW),
            pltpu.VMEM((2 * own, R), LOW),
            pltpu.VMEM((B, 5 * R, group), LOW),
            dma((2,)),
            *[dma((NP, CHUNKS))] * 4,
            *[dma((Z + 2,))] * 2,
            *[dma((Y,))] * 2,
            *[dma((NP + 1,))] * 4,
            *[dma] * 8,
        ]
        return pl.pallas_call(
            functools.partial(kernel, Y, Z, B, clusters),
            out_shape=(
                pltpu.VMEM((1, part, B * W), F32),
                pltpu.VMEM((group, R), F32),
            ),
            in_specs=[pl.BlockSpec(memory_space=pltpu.HBM)] * 2,
            out_specs=(pl.BlockSpec(memory_space=pltpu.VMEM),) * 2,
            scratch_shapes=scratch,
            compiler_params=pltpu.CompilerParams(
                collective_id=0, has_side_effects=True, vmem_limit_bytes=60 * 2**20
            ),
        )(profiles, assign.reshape(1, -1))

    return jax.shard_map(
        shards,
        mesh=mesh,
        in_specs=(P("doc", "bin"), P("doc")),
        out_specs=(P("bin", "doc", None), P("bin", "doc")),
        check_vma=False,
    )


def solution(mesh):
    return program(mesh, DEPTH, 4096)
```
